512 devices in a mesh: prompt: 16 (over y_hi, x, core), resp: 32 (over y_lo, z).
Axes of the slice: x: 4, y: 4 (y_hi: 2, y_lo: 2; y = y_hi * 2 + y_lo), z: 16, core: 2. Of those that a mesh axis runs over, the one named last changes fastest.
Arguments:
- query_prompt: bfloat16 [16, 1024, 2048], P('prompt', 'resp'), may hold values from -5 to 5
- query_resp: bfloat16 [16, 4096, 2048], P('prompt', 'resp'), may hold values from -6 to 6
- kv_prompt: bfloat16 [16, 1024, 1024], P('prompt', 'resp'), may hold values from -5 to 5
- kv_resp: bfloat16 [16, 4096, 1024], P('prompt', 'resp'), may hold values from -6 to 6
- grad_prompt: bfloat16 [16, 1024, 2048], P('prompt', 'resp'), may hold values from -24 to 24
- grad_resp: bfloat16 [16, 4096, 2048], P('prompt', 'resp'), may hold values from -24 to 24
- norm_gains: float32 [2, 128], replicated, may hold values from 0.5 to 4.5
- resp_lengths: int32 [16, 17], P('prompt'), may hold values from 1 to 1024, 4096 in all within a row
Outputs:
- dq_prompt: bfloat16 [16, 1024, 2048], P('prompt', 'resp')
- dq_resp: bfloat16 [16, 4096, 2048], P('prompt', 'resp')
- dkv_prompt: bfloat16 [16, 1024, 1024], P('prompt', 'resp')
- dkv_resp: bfloat16 [16, 4096, 1024], P('prompt', 'resp')
- norm_grads: float32 [2, 128], replicated
The draws below stay inside these ranges and needn't reach their ends.
Inputs may be any that keep to these rules, and one draw needn't show every extreme that they name: `resp_lengths`: each group's lengths sum to 4096; the largest is exactly 1024.
All inputs are finite; a program needn't handle non-finite values.
Results may differ from the reference program's by a relative error of at most 0.03.
The reference program's roundings to bfloat16 on the way (of `probs_low`, `out_low` and `ds_low`) count: a program that leaves them out, or rounds other values in their place, can miss the bound.
Values may be sent and summed in bfloat16 or wider, within the bound.
A program may use at most 128 MiB of HBM per device.

```python
import math
import jax
import jax.numpy as jnp
import numpy as np
from jax import lax

QHEADS = 16
KVHEADS = 4
HEADDIM = 128
SHARING = 4
PROMPT = 1024
RESP_DEV = 128
REACH = 8
RESPONSES = 17
LONGEST = 1024
RESP_TOKENS = 4096
GROUPS = 16
N_RESP = 32


def shared_keys(key):
    return jnp.clip(jax.random.normal(key, (GROUPS, PROMPT, KVHEADS, HEADDIM), jnp.float32), -4.0, 4.0)


def scaled_upstream(key, rows):
    first = jax.random.fold_in(key, 0)
    group_rise = 1.0 + jnp.arange(GROUPS, dtype=jnp.float32) / GROUPS
    row_rise = 1.0 + 2.0 * jnp.arange(rows, dtype=jnp.float32) / rows
    scale = group_rise[:, None, None] * row_rise[None, :, None]
    shape = (GROUPS, rows, QHEADS * HEADDIM)
    values = jnp.clip(jax.random.normal(first, shape, jnp.float32), -4.0, 4.0) * scale
    return values.astype(jnp.bfloat16)


def draw_kv_prompt(key, part):
    base = shared_keys(key)
    key = jax.random.fold_in(key, 3)
    second = jax.random.fold_in(key, 1)
    keys_part = base
    values = jnp.clip(jax.random.normal(second, (GROUPS, PROMPT, KVHEADS * HEADDIM), jnp.float32), -4.0, 4.0)
    return jnp.concatenate([keys_part.reshape(GROUPS, PROMPT, KVHEADS * HEADDIM), values], axis=2).astype(jnp.bfloat16)


def draw_query_prompt(key, part):
    key = jax.random.fold_in(key, 5)
    fresh = jnp.clip(jax.random.normal(key, (GROUPS, PROMPT, KVHEADS, SHARING, HEADDIM), jnp.float32), -4.0, 4.0)
    return fresh.reshape(GROUPS, PROMPT, QHEADS * HEADDIM).astype(jnp.bfloat16)


def draw_norm_gains(key, part):
    key = jax.random.fold_in(key, 7)
    return jax.random.uniform(key, (2, HEADDIM), jnp.float32, 0.6, 1.5)


def draw_grad_prompt(key, part):
    key = jax.random.fold_in(key, 9)
    return scaled_upstream(key, PROMPT)


def draw_grad_resp(key, part):
    key = jax.random.fold_in(key, 11)
    return scaled_upstream(key, RESP_TOKENS)


def block_scale(stream_key, dims, cuts, least, top_value):
    loudness = 1.0
    for dim, shards_of in cuts:
        steps = jax.random.uniform(jax.random.fold_in(jax.random.fold_in(stream_key, 6), dim), (shards_of,), jnp.float32, least / len(cuts), top_value / len(cuts))
        loudness = loudness * jnp.repeat(jnp.exp(steps), dims[dim] // shards_of).reshape((-1,) + (1,) * (len(dims) - 1 - dim))
    return loudness


def profile(count, total, reach, skew):
    loads = [(1 << 20) // math.isqrt(rank ** skew) + 1 for rank in range(2, count + 1)]
    rest, given = total - reach - (count - 1), [1] * (count - 1)
    while rest > 0:
        candidates = [i for i in range(count - 1) if given[i] < reach]
        mass, left = sum([loads[i] for i in candidates]), rest
        for i in candidates:
            extra = min(reach - given[i], max(1, left * loads[i] // mass), rest)
            given[i] = given[i] + extra
            rest = rest - extra
    return np.array([reach] + given)


def ragged_sizes(rng, count, total, reach, lean):
    if count == 2:
        one = jax.random.randint(rng, (), max(1, total - reach), min(reach, total - 1) + 1)
        return jnp.stack([one, total - one])
    sizes = jnp.asarray(profile(count, total, reach, lean), jnp.int32)
    twos = (count - 1) // 2
    giver, sink = sizes[1:1 + 2 * twos:2], sizes[2:2 + 2 * twos:2]
    room = jnp.minimum(giver - 1, reach - sink)
    moved = jax.random.randint(jax.random.fold_in(rng, 1), (twos,), 0, 1 << 20) % (room + 1)
    sizes = sizes.at[1:1 + 2 * twos:2].set(giver - moved).at[2:2 + 2 * twos:2].set(sink + moved)
    return sizes[jax.random.permutation(jax.random.fold_in(rng, 2), count)]


def centred(rng, shape, spread, limit, cuts=(), kind=jnp.bfloat16):
    drawn = jax.random.normal(rng, shape, jnp.float32) * spread
    if len(cuts) > 0:
        drawn = block_scale(rng, shape, cuts, -0.22, 0.18) * drawn
    return jnp.clip(drawn, min=-limit, max=limit).astype(kind)


def setup_inputs(seed: int = 0) -> dict:
    seeds = jax.random.split(jax.random.key(seed), 9)
    query_prompt = draw_query_prompt(jax.random.fold_in(seeds[8], 71), 0)
    query_resp = centred(seeds[1], (GROUPS, RESP_TOKENS, QHEADS * HEADDIM), 1.0, 6.0, ((0, 16), (1, 32)))
    kv_prompt = draw_kv_prompt(jax.random.fold_in(seeds[8], 71), 0)
    kv_resp = centred(seeds[3], (GROUPS, RESP_TOKENS, 2 * KVHEADS * HEADDIM), 1.0, 6.0, ((0, 16), (1, 32)))
    grad_prompt = draw_grad_prompt(jax.random.fold_in(seeds[8], 71), 0)
    grad_resp = draw_grad_resp(jax.random.fold_in(seeds[8], 71), 0)
    norm_gains = draw_norm_gains(jax.random.fold_in(seeds[8], 71), 0)
    resp_lengths = jax.vmap(lambda own: ragged_sizes(own, RESPONSES, RESP_TOKENS, LONGEST, 1))(jax.random.split(seeds[7], GROUPS)).reshape((GROUPS, RESPONSES)).astype(jnp.int32)
    return dict(query_prompt=query_prompt, query_resp=query_resp, kv_prompt=kv_prompt, kv_resp=kv_resp, grad_prompt=grad_prompt, grad_resp=grad_resp, norm_gains=norm_gains, resp_lengths=resp_lengths)


epsilon = 1e-06

def normalize(raw, gain, heads):
    values = raw.astype(jnp.float32).reshape(raw.shape[0], heads, HEADDIM)
    factor = lax.rsqrt(lax.optimization_barrier(jnp.mean(values * values, axis=-1, keepdims=True)) + epsilon)
    normed = values * factor
    return ((normed * gain).astype(jnp.bfloat16), normed, factor)

def norm_back(upstream, normed, factor, gain):
    scaled = upstream * gain
    inner = lax.optimization_barrier(jnp.mean(scaled * normed, axis=-1, keepdims=True))
    return (factor * (scaled - normed * inner), lax.optimization_barrier(jnp.sum(upstream * normed, axis=(0, 1))))

def grouped(array):
    return array.reshape(array.shape[0], KVHEADS, SHARING, HEADDIM)

def segment_of(index, ends):
    return lax.optimization_barrier(jnp.sum((index[:, None] >= ends[None, :]).astype(jnp.int32), axis=1))

def resp_mask(query_index, key_index, ends):
    same = segment_of(query_index, ends)[:, None] == segment_of(key_index, ends)[None, :]
    return (key_index[None, :] >= 0) & same & (key_index[None, :] <= query_index[:, None])

def attend_back(queries, upstream, keys, values, allowed):
    scale = HEADDIM ** (-0.5)
    q_full = queries.astype(jnp.float32)
    u_full = upstream.astype(jnp.float32)
    k_full = keys.astype(jnp.float32)
    v_full = values.astype(jnp.float32)
    scores = jnp.einsum('rhgd,khd->rhgk', q_full, k_full) * scale
    scores = jnp.where(allowed[:, None, None, :], scores, -jnp.inf)
    top = lax.optimization_barrier(jnp.max(scores, axis=-1, keepdims=True))
    expo = jnp.exp(scores - top)
    probs = expo / lax.optimization_barrier(jnp.sum(expo, axis=-1, keepdims=True))
    probs_low = lax.optimization_barrier(probs.astype(jnp.bfloat16)).astype(jnp.float32)
    output = jnp.einsum('rhgk,khd->rhgd', probs_low, v_full)
    out_low = lax.optimization_barrier(output.astype(jnp.bfloat16)).astype(jnp.float32)
    delta = lax.optimization_barrier(jnp.sum(u_full * out_low, axis=-1, keepdims=True))
    grad_values = jnp.einsum('rhgk,rhgd->khd', probs_low, u_full)
    grad_probs = jnp.einsum('rhgd,khd->rhgk', u_full, v_full)
    ds_low = lax.optimization_barrier((probs * (grad_probs - delta)).astype(jnp.bfloat16)).astype(jnp.float32)
    grad_queries = scale * jnp.einsum('rhgk,khd->rhgd', ds_low, k_full)
    grad_keys = scale * jnp.einsum('rhgk,rhgd->khd', ds_low, q_full)
    return (grad_queries, grad_keys, grad_values)

def one_group(query_p, query_r, kv_p, kv_r, grad_p, grad_r, lengths, gains):
    width = KVHEADS * HEADDIM
    qn_p, qhat_p, qfac_p = normalize(query_p, gains[0], QHEADS)
    qn_r, qhat_r, qfac_r = normalize(query_r, gains[0], QHEADS)
    kn_p, khat_p, kfac_p = normalize(kv_p[:, :width], gains[1], KVHEADS)
    kn_r, khat_r, kfac_r = normalize(kv_r[:, :width], gains[1], KVHEADS)
    val_p = kv_p[:, width:].reshape(PROMPT, KVHEADS, HEADDIM)
    val_r = kv_r[:, width:].reshape(RESP_TOKENS, KVHEADS, HEADDIM)
    ends = jnp.cumsum(lengths).astype(jnp.int32)
    prompt_index = jnp.arange(PROMPT, dtype=jnp.int32)
    causal = prompt_index[:, None] >= prompt_index[None, :]
    dq_p, dk_p, dv_p = attend_back(grouped(qn_p), grouped(grad_p), kn_p, val_p, causal)
    margin = REACH * RESP_DEV
    window = (REACH + 1) * RESP_DEV
    key_pad = jnp.concatenate([jnp.zeros((margin, KVHEADS, HEADDIM), jnp.bfloat16), kn_r], axis=0)
    val_pad = jnp.concatenate([jnp.zeros((margin, KVHEADS, HEADDIM), jnp.bfloat16), val_r], axis=0)
    query_all = grouped(qn_r)
    grad_all = grouped(grad_r)

    def step(carry, block):
        dk_acc, dv_acc, dk_pad, dv_pad = carry
        start = (block * RESP_DEV).astype(jnp.int32)
        q_block = lax.dynamic_slice_in_dim(query_all, start, RESP_DEV, 0)
        u_block = lax.dynamic_slice_in_dim(grad_all, start, RESP_DEV, 0)
        k_window = lax.dynamic_slice_in_dim(key_pad, start, window, 0)
        v_window = lax.dynamic_slice_in_dim(val_pad, start, window, 0)
        query_index = start + jnp.arange(RESP_DEV, dtype=jnp.int32)
        key_index = start - margin + jnp.arange(window, dtype=jnp.int32)
        allowed = jnp.concatenate([jnp.ones((RESP_DEV, PROMPT), bool), resp_mask(query_index, key_index, ends)], axis=1)
        dq_b, dk_b, dv_b = attend_back(q_block, u_block, jnp.concatenate([kn_p, k_window], 0), jnp.concatenate([val_p, v_window], 0), allowed)
        dk_acc = dk_acc + dk_b[:PROMPT]
        dv_acc = dv_acc + dv_b[:PROMPT]
        dk_pad = lax.dynamic_update_slice_in_dim(dk_pad, lax.dynamic_slice_in_dim(dk_pad, start, window, 0) + dk_b[PROMPT:], start, 0)
        dv_pad = lax.dynamic_update_slice_in_dim(dv_pad, lax.dynamic_slice_in_dim(dv_pad, start, window, 0) + dv_b[PROMPT:], start, 0)
        return ((dk_acc, dv_acc, dk_pad, dv_pad), dq_b)
    start_carry = (dk_p, dv_p, jnp.zeros((margin + RESP_TOKENS, KVHEADS, HEADDIM), jnp.float32), jnp.zeros((margin + RESP_TOKENS, KVHEADS, HEADDIM), jnp.float32))
    blocks = jnp.arange(N_RESP, dtype=jnp.int32)
    final, dq_r = lax.scan(step, start_carry, blocks)
    dk_p, dv_p, dk_pad, dv_pad = final
    dq_r = dq_r.reshape(RESP_TOKENS, QHEADS, HEADDIM)
    dq_p = dq_p.reshape(PROMPT, QHEADS, HEADDIM)
    raw_qp, gain_qp = norm_back(dq_p, qhat_p, qfac_p, gains[0])
    raw_qr, gain_qr = norm_back(dq_r, qhat_r, qfac_r, gains[0])
    raw_kp, gain_kp = norm_back(dk_p, khat_p, kfac_p, gains[1])
    raw_kr, gain_kr = norm_back(dk_pad[margin:], khat_r, kfac_r, gains[1])
    out_qp = raw_qp.reshape(PROMPT, QHEADS * HEADDIM).astype(jnp.bfloat16)
    out_qr = raw_qr.reshape(RESP_TOKENS, QHEADS * HEADDIM).astype(jnp.bfloat16)
    out_kp = jnp.concatenate([raw_kp.reshape(PROMPT, width), dv_p.reshape(PROMPT, width)], axis=1).astype(jnp.bfloat16)
    out_kr = jnp.concatenate([raw_kr.reshape(RESP_TOKENS, width), dv_pad[margin:].reshape(RESP_TOKENS, width)], axis=1).astype(jnp.bfloat16)
    return (out_qp, out_qr, out_kp, out_kr, jnp.stack([gain_qp + gain_qr, gain_kp + gain_kr]))

def reference(query_prompt, query_resp, kv_prompt, kv_resp, grad_prompt, grad_resp, norm_gains, resp_lengths):

    def per_group(inputs):
        return one_group(*inputs, norm_gains)
    out_qp, out_qr, out_kp, out_kr, gain_parts = lax.map(per_group, (query_prompt, query_resp, kv_prompt, kv_resp, grad_prompt, grad_resp, resp_lengths))
    count = GROUPS * (PROMPT + RESP_TOKENS)
    scales = jnp.array([[(count * QHEADS) ** (-0.5)], [(count * KVHEADS) ** (-0.5)]], jnp.float32)
    return (out_qp, out_qr, out_kp, out_kr, lax.optimization_barrier(jnp.sum(gain_parts, axis=0)) * scales)
```

```python
import functools

import jax
import jax.numpy as jnp
from jax import lax
from jax.experimental import pallas as pl
from jax.experimental.pallas import tpu as pltpu
from jax.sharding import PartitionSpec as P

MESH = pl.DeviceIdType.MESH
KH = 4
SH = 4
HD = 128
EPS = 1e-06
SCALE = HD ** (-0.5)
LOG2E = 1.4426950408889634
RROWS = 128
PROWS = 32
REACH = 8
NZ = 16
RC = SH * RROWS
PC = SH * PROWS
COLS = RC + PC
MASKED = -1e30
BF = jnp.bfloat16
F32 = jnp.float32


def dot(a, b):
    return lax.dot_general(a, b, (((1,), (0,)), ((), ())), preferred_element_type=F32)


def rms(x):
    factor = lax.rsqrt(jnp.mean(x * x, axis=-1, keepdims=True) + EPS)
    return x * factor, factor


def flip(index, bit):
    return index + (1 - 2 * ((index // bit) % 2)) * bit


def kernel(
    bits,
    total_rows,
    qp, qr, kvp, kvr, gp, gr, gains, lens,
    dqp, dqr, dkvp, dkvr, ngrad,
    win, pg, retr, rets, zr, zs, yr, ys, fin,
    qn, qt, do, dt, dqt, ew, dw, ep, dp,
    mref, lref, aref, mw, mp, red, redr,
    fs, fr, bs, br, azs, azr, ays, ayr, rzs, rzr, rys, ryr, rds, rdr,
):
    me = lax.axis_index("resp")
    pr = lax.axis_index("prompt")
    y = me // NZ
    z = me % NZ
    nxt = (me + 1) % (2 * NZ)
    prv = (me + 2 * NZ - 1) % (2 * NZ)
    znx = y * NZ + (z + 1) % NZ
    zpv = y * NZ + (z + NZ - 1) % NZ
    yp = (me + NZ) % (2 * NZ)

    partners = []
    for axis, bit in bits:
        if axis == "resp":
            partners.append((pr, flip(me, bit)))
        else:
            partners.append((flip(pr, bit), me))
    friends = [(pr, nxt), (pr, prv), (pr, znx), (pr, zpv), (pr, yp)] + partners

    barrier = pltpu.get_barrier_semaphore()
    for friend in friends:
        pl.semaphore_signal(barrier, inc=1, device_id=friend, device_id_type=MESH)

    g0 = gains[0:1, :]
    g1 = gains[1:2, :]

    def remote(src, dst, ssem, rsem, resp):
        return pltpu.make_async_remote_copy(
            src_ref=src, dst_ref=dst, send_sem=ssem, recv_sem=rsem,
            device_id=(pr, resp), device_id_type=MESH,
        )

    def fwd(k, h):
        return remote(win.at[k, h], win.at[k + 1, h], fs.at[k, h], fr.at[k, h], nxt)

    def back(k, h):
        return remote(rets.at[k - 1, h], retr.at[k - 1, h], bs.at[k - 1, h], br.at[k - 1, h], prv)

    def gather_z(t):
        return remote(pg.at[t, 0], pg.at[t + 1, 0], azs.at[t], azr.at[t], zpv)

    def gather_y(t):
        return remote(pg.at[t, 0], pg.at[t, 1], ays.at[t], ayr.at[t], yp)

    def scatter_z(t):
        return remote(zs.at[t - 1], zr.at[t - 1], rzs.at[t - 1], rzr.at[t - 1], znx)

    def scatter_y(t):
        return remote(ys.at[t], yr.at[t], rys.at[t], ryr.at[t], yp)

    for h in range(KH):
        cols = slice(h * HD, (h + 1) * HD)
        vcols = slice((KH + h) * HD, (KH + h + 1) * HD)
        khat, _ = rms(kvr[:, cols].astype(F32))
        win[0, h, :, 0:HD] = (khat * g1).astype(BF)
        win[0, h, :, HD : 2 * HD] = kvr[:, vcols]
        khat, _ = rms(kvp[:, cols].astype(F32))
        pg[0, 0, h, :, 0:HD] = (khat * g1).astype(BF)
        pg[0, 0, h, :, HD : 2 * HD] = kvp[:, vcols]

    pl.semaphore_wait(barrier, len(friends))
    gather_z(0).start()
    gather_y(0).start()
    for h in range(KH):
        fwd(0, h).start()

    for h in range(KH):
        for g in range(SH):
            head = h * SH + g
            cols = slice(head * HD, (head + 1) * HD)
            rows = slice(g * RROWS, (g + 1) * RROWS)
            prows = slice(RC + g * PROWS, RC + (g + 1) * PROWS)
            qhat, _ = rms(qr[:, cols].astype(F32))
            low = (qhat * g0).astype(BF)
            qn[h, rows, :] = low
            qt[h, :, rows] = low.astype(F32).T.astype(BF)
            qhat, _ = rms(qp[:, cols].astype(F32))
            qn[h, prows, :] = (qhat * g0).astype(BF)
            do[h, rows, :] = gr[:, cols]
            dt[h, :, rows] = gr[:, cols].astype(F32).T.astype(BF)
            do[h, prows, :] = gp[:, cols]
        qt[h, :, RC:COLS] = qn[h, RC:COLS, :].astype(F32).T.astype(BF)
        dt[h, :, RC:COLS] = do[h, RC:COLS, :].astype(F32).T.astype(BF)
        dqt[h] = jnp.zeros((HD, COLS), F32)

    lane = lax.broadcasted_iota(jnp.int32, (1, RC), 1)
    row_index = me * RROWS + lane % RROWS
    first = jnp.zeros((1, RC), jnp.int32)
    end = jnp.int32(0)
    for j in range(lens.shape[1]):
        end = end + lens[0, j]
        first = jnp.where(row_index >= end, end, first)

    def online(keys, vals, h, lo, hi, allowed, eref, dref, mold, lold, aold):
        cols = slice(lo, hi)
        scores = dot(keys, qt[h, :, cols]) * (SCALE * LOG2E)
        probs_grad = dot(vals, dt[h, :, cols])
        if allowed is not None:
            scores = jnp.where(allowed, scores, MASKED)
        top = jnp.maximum(mold, jnp.max(scores, axis=0, keepdims=True))
        shrink = jnp.exp2(mold - top)
        expo = jnp.exp2(scores - top)
        mref[h, :, cols] = top
        lref[h, :, cols] = lold * shrink + jnp.sum(expo, axis=0, keepdims=True)
        aref[h, :, cols] = aold * shrink + jnp.sum(expo * probs_grad, axis=0, keepdims=True)
        eref[:, cols] = expo
        dref[:, cols] = probs_grad
        return top

    def old(h, lo, hi):
        return mref[h, :, lo:hi], lref[h, :, lo:hi], aref[h, :, lo:hi]

    def key_rows(k):
        return (me - k) * RROWS + lax.broadcasted_iota(jnp.int32, (RROWS, RC), 0)

    def window_keys(k, h):
        return win[k, h, :, 0:HD], win[k, h, :, HD : 2 * HD]

    def forward_own(h):
        keys, vals = window_keys(0, h)
        index = key_rows(0)
        allowed = (index >= first) & (index <= row_index)
        start = jnp.full((1, RC), MASKED, F32)
        zero = jnp.zeros((1, RC), F32)
        top = online(keys, vals, h, 0, RC, allowed, ew.at[0, h], dw.at[0, h], start, zero, zero)
        mw[0, h] = top
        mref[h, :, RC:COLS] = jnp.full((1, PC), MASKED, F32)
        lref[h, :, RC:COLS] = jnp.zeros((1, PC), F32)
        aref[h, :, RC:COLS] = jnp.zeros((1, PC), F32)

    def forward_window(k, h):
        keys, vals = window_keys(k, h)
        allowed = key_rows(k) >= first
        mw[k, h] = online(keys, vals, h, 0, RC, allowed, ew.at[k, h], dw.at[k, h], *old(h, 0, RC))

    def prompt_keys(j, h):
        keys = pg[pl.ds(2 * j, 2), :, h, :, 0:HD].reshape(4 * PROWS, HD)
        vals = pg[pl.ds(2 * j, 2), :, h, :, HD : 2 * HD].reshape(4 * PROWS, HD)
        return keys, vals

    def forward_prompt(j, h):
        keys, vals = prompt_keys(j, h)
        sub = lax.broadcasted_iota(jnp.int32, (4 * PROWS, PC), 0)
        ring = jnp.where((sub & 32) == 0, y, 1 - y)
        chip = (z + 2 * j + (sub >> 6)) & (NZ - 1)
        position = (ring * NZ + chip) * PROWS + (sub & 31)
        query = me * PROWS + (lax.broadcasted_iota(jnp.int32, (4 * PROWS, PC), 1) & 31)
        er, dr = ep.at[j, h], dp.at[j, h]
        mp[j, h, :, 0:RC] = online(keys, vals, h, 0, RC, None, er, dr, *old(h, 0, RC))
        mp[j, h, :, RC:COLS] = online(
            keys, vals, h, RC, COLS, position <= query, er, dr, *old(h, RC, COLS)
        )

    def loop(count, body):
        def step(i, carry):
            body(i)
            return carry

        lax.fori_loop(0, count, step, 0)

    loop(KH, forward_own)

    def forward_step(n):
        k = n // KH
        h = n % KH
        fwd(k, h).wait_recv()

        @pl.when(k < REACH - 1)
        def _():
            fwd(k + 1, h).start()

        t = 2 * k + 1 + h // 2

        @pl.when((h % 2 == 0) & (t < NZ))
        def _():
            gather_z(t - 1).wait_recv()
            gather_y(t).start()

            @pl.when(t < NZ - 1)
            def _():
                gather_z(t).start()

        forward_window(k + 1, h)

        @pl.when(k >= 1)
        def _():
            @pl.when(h == 0)
            def _():
                gather_y(2 * k - 2).wait_recv()
                gather_y(2 * k - 1).wait_recv()

            forward_prompt(k - 1, h)

    loop(KH * REACH, forward_step)
    gather_y(NZ - 2).wait_recv()
    gather_y(NZ - 1).wait_recv()
    loop(KH, lambda h: forward_prompt(NZ // 2 - 1, h))

    def finish(h):
        inverse = 1.0 / lref[h]
        lref[h] = inverse
        aref[h] = aref[h] * inverse

    loop(KH, finish)

    def backward(keys, h, hi, top, eref, dref):
        weight = jnp.exp2(top - mref[h, :, 0:hi]) * lref[h, :, 0:hi]
        probs = eref[:, 0:hi] * weight
        low = probs.astype(BF)
        ds = (probs * (dref[:, 0:hi] - aref[h, :, 0:hi])).astype(BF)
        dk = dot(ds, qn[h, 0:hi, :]) * SCALE
        dv = dot(low, do[h, 0:hi, :])
        dqt[h, :, 0:hi] += dot(keys.astype(F32).T.astype(BF), ds)
        return dk, dv

    def backward_window(k, h):
        dk, dv = backward(window_keys(k, h)[0], h, RC, mw[k, h], ew.at[k, h], dw.at[k, h])
        ew[k, h, :, 0:HD] = dk
        ew[k, h, :, HD : 2 * HD] = dv

    def backward_prompt(j, h):
        dk, dv = backward(prompt_keys(j, h)[0], h, COLS, mp[j, h], ep.at[j, h], dp.at[j, h])
        ep[j, h, :, 0:HD] = dk
        ep[j, h, :, HD : 2 * HD] = dv
        for i in range(2):
            part = slice((2 * i + 1) * PROWS, (2 * i + 2) * PROWS)
            ys[2 * j + i, h, :, 0:HD] = dk[part].astype(BF)
            ys[2 * j + i, h, :, HD : 2 * HD] = dv[part].astype(BF)

    def return_first(h):
        backward_window(REACH, h)
        rets[REACH - 1, h] = ew[REACH, h, :, 0 : 2 * HD].astype(BF)
        back(REACH, h).start()

    loop(KH, return_first)

    def return_hop(k, h):
        back(k + 1, h).wait_recv()
        rets[k - 1, h] = (ew[k, h, :, 0 : 2 * HD] + retr[k, h].astype(F32)).astype(BF)
        back(k, h).start()

    def ring_sum(t):
        j = t // 2
        at = pl.multiple_of((t % 2) * (2 * PROWS), 2 * PROWS)
        return ep[j, :, pl.ds(at, PROWS), 0 : 2 * HD] + yr[t].astype(F32)

    def ring_first():
        scatter_y(NZ - 1).wait_recv()
        zs[NZ - 2] = ring_sum(NZ - 1).astype(BF)
        scatter_z(NZ - 1).start()

    def ring_hop(t):
        scatter_y(t).wait_recv()
        scatter_z(t + 1).wait_recv()
        zs[t - 1] = (ring_sum(t) + zr[t].astype(F32)).astype(BF)
        scatter_z(t).start()

    def ring_last():
        scatter_y(0).wait_recv()
        scatter_z(1).wait_recv()
        fin[...] = ring_sum(0) + zr[0].astype(F32)

    def return_step(n):
        s = 1 + n // KH
        h = n % KH
        backward_window(REACH + 1 - 2 * s, h)
        return_hop(REACH - s, h)
        backward_window(REACH - 2 * s, h)
        hop = NZ - 1 - (3 * (s - 2) + h)

        @pl.when((n == KH))
        def _():
            ring_first()

        @pl.when((n > KH) & (h < 3))
        def _():
            ring_hop(hop)

        j = NZ // 2 + 1 - 2 * s
        backward_prompt(j, h)
        backward_prompt(j - 1, h)

        @pl.when(h == KH - 1)
        def _():
            for i in range(4):
                scatter_y(2 * j + 1 - i).start()

    loop(KH * (REACH // 2), return_step)

    part = jnp.zeros((1, HD), F32)

    def query_back(raw, upstream):
        qhat, factor = rms(raw.astype(F32))
        u = upstream * g0
        inner = jnp.mean(u * qhat, axis=-1, keepdims=True)
        return factor * (u - qhat * inner), jnp.sum(upstream * qhat, axis=0, keepdims=True)

    for h in range(KH):
        tail = dqt[h, :, RC:COLS].T * SCALE
        for g in range(SH):
            head = h * SH + g
            cols = slice(head * HD, (head + 1) * HD)
            upstream = dqt[h, :, g * RROWS : (g + 1) * RROWS].T * SCALE
            out, more = query_back(qr[:, cols], upstream)
            dqr[:, cols] = out.astype(BF)
            part = part + more
            out, more = query_back(qp[:, cols], tail[g * PROWS : (g + 1) * PROWS])
            dqp[:, cols] = out.astype(BF)
            part = part + more
    red[0] = jnp.broadcast_to(part, (8, HD))

    def gain_copy(i):
        return pltpu.make_async_remote_copy(
            src_ref=red.at[i], dst_ref=redr.at[i], send_sem=rds.at[i], recv_sem=rdr.at[i],
            device_id=partners[i], device_id_type=MESH,
        )

    steps = len(partners)
    if steps:
        gain_copy(0).start()

    def gain_step(i):
        if i < steps:
            gain_copy(i).wait_recv()
            red[i + 1] = red[i] + redr[i]
            if i + 1 < steps:
                gain_copy(i + 1).start()

    done = 0
    for s in range(REACH // 2 + 1, REACH):
        for h in range(KH):
            return_hop(REACH - s, h)
            hop = NZ - 1 - (3 * (s - 2) + h)
            if h < 3 and hop > 0:
                ring_hop(hop)
            if h < 3 and hop == 0:
                ring_last()
            gain_step(done)
            done += 1
    while done < steps:
        gain_step(done)
        done += 1

    scales = [(total_rows * heads) ** (-0.5) for heads in (KH * SH, KH)]
    whole = red[steps][0:1, :]
    ngrad[0:1, :] = whole * scales[0]
    ngrad[1:2, :] = whole * (g0 / g1) * scales[1]

    def key_back(raw, upstream):
        khat, factor = rms(raw.astype(F32))
        u = upstream * g1
        inner = jnp.mean(u * khat, axis=-1, keepdims=True)
        return factor * (u - khat * inner)

    for h in range(KH):
        cols = slice(h * HD, (h + 1) * HD)
        vcols = slice((KH + h) * HD, (KH + h + 1) * HD)
        dkvp[:, cols] = key_back(kvp[:, cols], fin[h, :, 0:HD]).astype(BF)
        dkvp[:, vcols] = fin[h, :, HD : 2 * HD].astype(BF)
    for h in range(KH):
        cols = slice(h * HD, (h + 1) * HD)
        vcols = slice((KH + h) * HD, (KH + h + 1) * HD)
        back(1, h).wait_recv()
        own = ew[0, h, :, 0 : 2 * HD] + retr[0, h].astype(F32)
        dkvr[:, cols] = key_back(kvr[:, cols], own[:, 0:HD]).astype(BF)
        dkvr[:, vcols] = own[:, HD : 2 * HD].astype(BF)

    def sent(n):
        fwd(n // KH, n % KH).wait_send()
        back(n // KH + 1, n % KH).wait_send()

    loop(KH * REACH, sent)

    def ring_sent(t):
        gather_z(t).wait_send()
        scatter_z(t + 1).wait_send()
        gather_y(t).wait_send()
        scatter_y(t).wait_send()

    loop(NZ - 1, ring_sent)
    gather_y(NZ - 1).wait_send()
    scatter_y(NZ - 1).wait_send()
    for i in range(steps):
        gain_copy(i).wait_send()


def per_device(mesh_shape, qp, qr, kvp, kvr, gp, gr, gains, lens):
    bits = []
    for axis in ("resp", "prompt"):
        bit = 1
        while bit < mesh_shape[axis]:
            bits.append((axis, bit))
            bit *= 2
    total_rows = mesh_shape["prompt"] * mesh_shape["resp"] * (PROWS + RROWS)
    slots = max(1, len(bits))
    vmem = pl.BlockSpec(memory_space=pltpu.VMEM)
    dma = pltpu.SemaphoreType.DMA
    block = (KH, RROWS, 2 * HD)
    pblock = (KH, PROWS, 2 * HD)
    scratch = [
        pltpu.VMEM((REACH + 1,) + block, BF),
        pltpu.VMEM((NZ, 2) + pblock, BF),
        pltpu.VMEM((REACH,) + block, BF),
        pltpu.VMEM((REACH,) + block, BF),
        pltpu.VMEM((NZ - 1,) + pblock, BF),
        pltpu.VMEM((NZ - 1,) + pblock, BF),
        pltpu.VMEM((NZ,) + pblock, BF),
        pltpu.VMEM((NZ,) + pblock, BF),
        pltpu.VMEM(pblock, F32),
        pltpu.VMEM((KH, COLS, HD), BF),
        pltpu.VMEM((KH, HD, COLS), BF),
        pltpu.VMEM((KH, COLS, HD), BF),
        pltpu.VMEM((KH, HD, COLS), BF),
        pltpu.VMEM((KH, HD, COLS), F32),
        pltpu.VMEM((REACH + 1, KH, RROWS, RC), F32),
        pltpu.VMEM((REACH + 1, KH, RROWS, RC), F32),
        pltpu.VMEM((NZ // 2, KH, 4 * PROWS, COLS), F32),
        pltpu.VMEM((NZ // 2, KH, 4 * PROWS, COLS), F32),
        pltpu.VMEM((KH, 1, COLS), F32),
        pltpu.VMEM((KH, 1, COLS), F32),
        pltpu.VMEM((KH, 1, COLS), F32),
        pltpu.VMEM((REACH + 1, KH, 1, RC), F32),
        pltpu.VMEM((NZ // 2, KH, 1, COLS), F32),
        pltpu.VMEM((slots + 1, 8, HD), F32),
        pltpu.VMEM((slots, 8, HD), F32),
        dma((REACH, KH)), dma((REACH, KH)), dma((REACH, KH)), dma((REACH, KH)),
        dma((NZ - 1,)), dma((NZ - 1,)), dma((NZ,)), dma((NZ,)),
        dma((NZ - 1,)), dma((NZ - 1,)), dma((NZ,)), dma((NZ,)),
        dma((slots,)), dma((slots,)),
    ]
    width = qp.shape[2]
    kvwidth = kvp.shape[2]
    outs = pl.pallas_call(
        functools.partial(kernel, tuple(bits), total_rows),
        out_shape=(
            jax.ShapeDtypeStruct((PROWS, width), BF),
            jax.ShapeDtypeStruct((RROWS, width), BF),
            jax.ShapeDtypeStruct((PROWS, kvwidth), BF),
            jax.ShapeDtypeStruct((RROWS, kvwidth), BF),
            jax.ShapeDtypeStruct((2, HD), F32),
        ),
        in_specs=[vmem] * 7 + [pl.BlockSpec(memory_space=pltpu.SMEM)],
        out_specs=(vmem,) * 5,
        scratch_shapes=scratch,
        compiler_params=pltpu.CompilerParams(
            collective_id=0, has_side_effects=True, vmem_limit_bytes=62 * 1024 * 1024
        ),
    )(qp[0], qr[0], kvp[0], kvr[0], gp[0], gr[0], gains, lens)
    return outs[0][None], outs[1][None], outs[2][None], outs[3][None], outs[4]


def solution(mesh):
    rows = P("prompt", "resp", None)
    return jax.shard_map(
        functools.partial(per_device, dict(mesh.shape)),
        mesh=mesh,
        in_specs=(rows,) * 6 + (P(), P("prompt", None)),
        out_specs=(rows,) * 4 + (P(),),
        check_vma=False,
    )
```

```python
import functools

import jax
import jax.numpy as jnp
from jax import lax
from jax.experimental import pallas as pl
from jax.experimental.pallas import tpu as pltpu
from jax.sharding import PartitionSpec as P

MESH = pl.DeviceIdType.MESH
KH = 4
SH = 4
HD = 128
EPS = 1e-06
SCALE = HD ** (-0.5)
LOG2E = 1.4426950408889634
RROWS = 128
PROWS = 32
REACH = 8
NZ = 16
RC = SH * RROWS
PC = SH * PROWS
COLS = RC + PC
MASKED = -1e30
BF = jnp.bfloat16
F32 = jnp.float32


def dot(a, b):
    return lax.dot_general(a, b, (((1,), (0,)), ((), ())), preferred_element_type=F32)


def rms(x):
    factor = lax.rsqrt(jnp.mean(x * x, axis=-1, keepdims=True) + EPS)
    return x * factor, factor


def flip(index, bit):
    return index + (1 - 2 * ((index // bit) % 2)) * bit


def kernel(
    rounds,
    total_rows,
    qp, qr, kvp, kvr, gp, gr, gains, lens,
    dqp, dqr, dkvp, dkvr, ngrad,
    win, pg, retr, rets, zr, zs, yr, ys, sider, sides, fin,
    qn, qt, do, dt, dqt, ew, dw, ep, dp,
    mref, lref, aref, mw, mp, red, redr,
    fs, fr, fxs, bs, br, bxs, azs, azr, ays, ayr, rzs, rzr, rys, ryr, rxs, rxr, rds, rdr,
):
    me = lax.axis_index("resp")
    pr = lax.axis_index("prompt")
    y = me // NZ
    z = me % NZ
    nxt = (me + 1) % (2 * NZ)
    prv = (me + 2 * NZ - 1) % (2 * NZ)
    up1 = y * NZ + (z + 1) % NZ
    up2 = y * NZ + (z + 2) % NZ
    down1 = y * NZ + (z + NZ - 1) % NZ
    down2 = y * NZ + (z + NZ - 2) % NZ
    yp = (me + NZ) % (2 * NZ)

    def flipped(place, axis, bit):
        if axis == "prompt":
            return flip(place[0], bit), place[1]
        return place[0], flip(place[1], bit)

    partners = []
    for pair in rounds:
        places = [flipped((pr, me), *pair[0])]
        if len(pair) == 2:
            other = flipped((pr, me), *pair[1])
            places += [other, flipped(other, *pair[0])]
        partners.append(places)
    friends = [(pr, i) for i in (nxt, prv, up1, up2, down1, down2, yp)]
    for places in partners:
        friends += places

    barrier = pltpu.get_barrier_semaphore()
    for friend in friends:
        pl.semaphore_signal(barrier, inc=1, device_id=friend, device_id_type=MESH)

    g0 = gains[0:1, :]
    g1 = gains[1:2, :]

    def remote(src, dst, ssem, rsem, resp):
        return pltpu.make_async_remote_copy(
            src_ref=src, dst_ref=dst, send_sem=ssem, recv_sem=rsem,
            device_id=(pr, resp), device_id_type=MESH,
        )

    def onward(h, ring, row):
        return ring + (h // 2) * (row - ring)

    def fwd(k, h):
        to = onward(h, nxt, up1)
        return remote(win.at[k, h], win.at[k + 1, h], fs.at[k, h], fr.at[k, h], to)

    def fwd_over(k, h):
        return remote(win.at[k + 1, h], win.at[k + 1, h], fxs.at[k, h], fr.at[k, h], yp)

    def back(k, h):
        to = onward(h, prv, down1)
        i = k - 1
        return remote(rets.at[i, h], retr.at[i, h], bs.at[i, h], br.at[i, h], to)

    def back_over(k, h):
        i = k - 1
        return remote(retr.at[i, h], retr.at[i, h], bxs.at[i, h], br.at[i, h], yp)

    def fwd_sends(h):
        return (h < KH // 2) | (me != 2 * NZ - 1)

    def back_sends(h):
        return (h < KH // 2) | (me != 0)

    def fwd_start(k, h):
        @pl.when(fwd_sends(h))
        def _():
            fwd(k, h).start()

    def back_start(k, h):
        @pl.when(back_sends(h))
        def _():
            back(k, h).start()

    def fwd_arrived(k, h):
        fwd(k, h).wait_recv()

        @pl.when((h >= KH // 2) & (me == 0))
        def _():
            fwd_over(k, h).start()

    def back_arrived(k, h):
        back(k, h).wait_recv()

        @pl.when((h >= KH // 2) & (me == 2 * NZ - 1))
        def _():
            back_over(k, h).start()

    def returned(k, h):
        keep = jnp.where((h >= KH // 2) & (me == 2 * NZ - 1), 0.0, 1.0)
        return retr[k, h].astype(F32) * keep

    def gather_two(m):
        t = 2 * m
        return remote(pg.at[t, 0], pg.at[t + 2, 0], azs.at[t], azr.at[t], down2)

    def gather_one(m):
        t = 2 * m
        return remote(pg.at[t, 0], pg.at[t + 1, 0], azs.at[t + 1], azr.at[t + 1], down1)

    def gather_y(m):
        t = 2 * m
        return remote(pg.at[t, 0], pg.at[t, 1], ays.at[t], ayr.at[t], yp)

    def gather_side(m):
        t = 2 * m
        return remote(pg.at[t, 1], pg.at[t + 1, 1], ays.at[t + 1], ayr.at[t + 1], down1)

    def scatter_one(m):
        t = 2 * m
        return remote(zs.at[t], zr.at[t], rzs.at[t], rzr.at[t], up1)

    def scatter_two(m):
        t = 2 * m - 1
        return remote(zs.at[t], zr.at[t], rzs.at[t], rzr.at[t], up2)

    def scatter_side(m):
        return remote(sides.at[m], sider.at[m], rxs.at[m], rxr.at[m], up1)

    def scatter_y(m):
        return remote(ys.at[m], yr.at[m], rys.at[m], ryr.at[m], yp)

    for h in range(KH):
        cols = slice(h * HD, (h + 1) * HD)
        vcols = slice((KH + h) * HD, (KH + h + 1) * HD)
        khat, _ = rms(kvr[:, cols].astype(F32))
        win[0, h, :, 0:HD] = (khat * g1).astype(BF)
        win[0, h, :, HD : 2 * HD] = kvr[:, vcols]
        khat, _ = rms(kvp[:, cols].astype(F32))
        pg[0, 0, h, :, 0:HD] = (khat * g1).astype(BF)
        pg[0, 0, h, :, HD : 2 * HD] = kvp[:, vcols]

    pl.semaphore_wait(barrier, len(friends))
    gather_two(0).start()
    gather_one(0).start()
    gather_y(0).start()
    for h in range(KH):
        fwd_start(0, h)

    for h in range(KH):
        for g in range(SH):
            head = h * SH + g
            cols = slice(head * HD, (head + 1) * HD)
            rows = slice(g * RROWS, (g + 1) * RROWS)
            prows = slice(RC + g * PROWS, RC + (g + 1) * PROWS)
            qhat, _ = rms(qr[:, cols].astype(F32))
            low = (qhat * g0).astype(BF)
            qn[h, rows, :] = low
            qt[h, :, rows] = low.astype(F32).T.astype(BF)
            qhat, _ = rms(qp[:, cols].astype(F32))
            qn[h, prows, :] = (qhat * g0).astype(BF)
            do[h, rows, :] = gr[:, cols]
            dt[h, :, rows] = gr[:, cols].astype(F32).T.astype(BF)
            do[h, prows, :] = gp[:, cols]
        qt[h, :, RC:COLS] = qn[h, RC:COLS, :].astype(F32).T.astype(BF)
        dt[h, :, RC:COLS] = do[h, RC:COLS, :].astype(F32).T.astype(BF)
        dqt[h] = jnp.zeros((HD, COLS), F32)

    lane = lax.broadcasted_iota(jnp.int32, (1, RC), 1)
    row_index = me * RROWS + lane % RROWS
    first = jnp.zeros((1, RC), jnp.int32)
    end = jnp.int32(0)
    for j in range(lens.shape[1]):
        end = end + lens[0, j]
        first = jnp.where(row_index >= end, end, first)

    def online(keys, vals, h, lo, hi, allowed, eref, dref, mold, lold, aold):
        cols = slice(lo, hi)
        scores = dot(keys, qt[h, :, cols]) * (SCALE * LOG2E)
        probs_grad = dot(vals, dt[h, :, cols])
        if allowed is not None:
            scores = jnp.where(allowed, scores, MASKED)
        top = jnp.maximum(mold, jnp.max(scores, axis=0, keepdims=True))
        shrink = jnp.exp2(mold - top)
        expo = jnp.exp2(scores - top)
        mref[h, :, cols] = top
        lref[h, :, cols] = lold * shrink + jnp.sum(expo, axis=0, keepdims=True)
        aref[h, :, cols] = aold * shrink + jnp.sum(expo * probs_grad, axis=0, keepdims=True)
        eref[:, cols] = expo
        dref[:, cols] = probs_grad
        return top

    def old(h, lo, hi):
        return mref[h, :, lo:hi], lref[h, :, lo:hi], aref[h, :, lo:hi]

    def key_rows(k):
        return (me - k) * RROWS + lax.broadcasted_iota(jnp.int32, (RROWS, RC), 0)

    def window_keys(k, h):
        return win[k, h, :, 0:HD], win[k, h, :, HD : 2 * HD]

    def forward_own(h):
        keys, vals = window_keys(0, h)
        index = key_rows(0)
        allowed = (index >= first) & (index <= row_index)
        start = jnp.full((1, RC), MASKED, F32)
        zero = jnp.zeros((1, RC), F32)
        top = online(keys, vals, h, 0, RC, allowed, ew.at[0, h], dw.at[0, h], start, zero, zero)
        mw[0, h] = top
        mref[h, :, RC:COLS] = jnp.full((1, PC), MASKED, F32)
        lref[h, :, RC:COLS] = jnp.zeros((1, PC), F32)
        aref[h, :, RC:COLS] = jnp.zeros((1, PC), F32)

    def forward_window(k, h):
        keys, vals = window_keys(k, h)
        allowed = key_rows(k) >= first
        mw[k, h] = online(keys, vals, h, 0, RC, allowed, ew.at[k, h], dw.at[k, h], *old(h, 0, RC))

    def prompt_keys(j, h):
        keys = pg[pl.ds(2 * j, 2), :, h, :, 0:HD].reshape(4 * PROWS, HD)
        vals = pg[pl.ds(2 * j, 2), :, h, :, HD : 2 * HD].reshape(4 * PROWS, HD)
        return keys, vals

    def forward_prompt(j, h):
        keys, vals = prompt_keys(j, h)
        sub = lax.broadcasted_iota(jnp.int32, (4 * PROWS, PC), 0)
        ring = jnp.where((sub & 32) == 0, y, 1 - y)
        chip = (z + 2 * j + (sub >> 6)) & (NZ - 1)
        position = (ring * NZ + chip) * PROWS + (sub & 31)
        query = me * PROWS + (lax.broadcasted_iota(jnp.int32, (4 * PROWS, PC), 1) & 31)
        er, dr = ep.at[j, h], dp.at[j, h]
        mp[j, h, :, 0:RC] = online(keys, vals, h, 0, RC, None, er, dr, *old(h, 0, RC))
        mp[j, h, :, RC:COLS] = online(
            keys, vals, h, RC, COLS, position <= query, er, dr, *old(h, RC, COLS)
        )

    def loop(count, body):
        def step(i, carry):
            body(i)
            return carry

        lax.fori_loop(0, count, step, 0)

    loop(KH, forward_own)

    def forward_step(n):
        k = n // KH
        h = n % KH
        fwd_arrived(k, h)

        @pl.when(k < REACH - 1)
        def _():
            fwd_start(k + 1, h)

        @pl.when((n % 3 == 2) & (n < 3 * (NZ // 2)))
        def _():
            m = n // 3

            @pl.when(m < NZ // 2 - 1)
            def _():
                gather_two(m).wait_recv()

                @pl.when(m < NZ // 2 - 2)
                def _():
                    gather_two(m + 1).start()

                gather_one(m + 1).start()
                gather_y(m + 1).start()

            gather_y(m).wait_recv()
            gather_side(m).start()

        forward_window(k + 1, h)

        @pl.when(k >= 1)
        def _():
            @pl.when(h == 0)
            def _():
                gather_one(k - 1).wait_recv()
                gather_side(k - 1).wait_recv()

            forward_prompt(k - 1, h)

        @pl.when(k == REACH - 1)
        def _():
            @pl.when(h == 0)
            def _():
                gather_one(NZ // 2 - 1).wait_recv()
                gather_side(NZ // 2 - 1).wait_recv()

            forward_prompt(NZ // 2 - 1, h)

    loop(KH * REACH, forward_step)

    def finish(h):
        inverse = 1.0 / lref[h]
        lref[h] = inverse
        aref[h] = aref[h] * inverse

    loop(KH, finish)

    def backward(keys, h, hi, top, eref, dref):
        weight = jnp.exp2(top - mref[h, :, 0:hi]) * lref[h, :, 0:hi]
        probs = eref[:, 0:hi] * weight
        low = probs.astype(BF)
        ds = (probs * (dref[:, 0:hi] - aref[h, :, 0:hi])).astype(BF)
        dk = dot(ds, qn[h, 0:hi, :]) * SCALE
        dv = dot(low, do[h, 0:hi, :])
        dqt[h, :, 0:hi] += dot(keys.astype(F32).T.astype(BF), ds)
        return dk, dv

    def backward_window(k, h):
        dk, dv = backward(window_keys(k, h)[0], h, RC, mw[k, h], ew.at[k, h], dw.at[k, h])
        ew[k, h, :, 0:HD] = dk
        ew[k, h, :, HD : 2 * HD] = dv

    def backward_prompt(j, h):
        dk, dv = backward(prompt_keys(j, h)[0], h, COLS, mp[j, h], ep.at[j, h], dp.at[j, h])
        ep[j, h, :, 0:HD] = dk
        ep[j, h, :, HD : 2 * HD] = dv
        sides[j, h, :, 0:HD] = dk[3 * PROWS :].astype(BF)
        sides[j, h, :, HD : 2 * HD] = dv[3 * PROWS :].astype(BF)

    def return_first(h):
        backward_window(REACH, h)
        rets[REACH - 1, h] = ew[REACH, h, :, 0 : 2 * HD].astype(BF)
        back_start(REACH, h)

    loop(KH, return_first)

    def return_hop(k, h):
        back_arrived(k + 1, h)
        rets[k - 1, h] = (ew[k, h, :, 0 : 2 * HD] + returned(k, h)).astype(BF)
        back_start(k, h)

    def prompt_part(j, quarter):
        return ep[j, :, quarter * PROWS : (quarter + 1) * PROWS, 0 : 2 * HD]

    def ring_odd(m):
        zs[2 * m] = prompt_part(m, 2).astype(BF)
        scatter_one(m).start()
        scatter_side(m).start()

    def ring_cross(m):
        scatter_side(m).wait_recv()
        ys[m] = (prompt_part(m, 1) + sider[m].astype(F32)).astype(BF)
        scatter_y(m).start()

    def ring_even(m):
        scatter_y(m).wait_recv()
        scatter_one(m).wait_recv()
        return prompt_part(m, 0) + yr[m].astype(F32) + zr[2 * m].astype(F32)

    def ring_first():
        m = NZ // 2 - 1
        zs[2 * m - 1] = ring_even(m).astype(BF)
        scatter_two(m).start()

    def ring_hop(m):
        total = ring_even(m)
        scatter_two(m + 1).wait_recv()
        zs[2 * m - 1] = (total + zr[2 * m + 1].astype(F32)).astype(BF)
        scatter_two(m).start()

    def ring_last():
        total = ring_even(0)
        scatter_two(1).wait_recv()
        fin[...] = total + zr[1].astype(F32)

    def return_step(n):
        s = 1 + n // KH
        h = n % KH

        @pl.when(s > 1)
        def _():
            return_hop(REACH - s, h)

        @pl.when((n >= 4) & (n % 2 == 0))
        def _():
            ring_cross(NZ // 2 - 1 - (n - 4) // 2)

        @pl.when(n == 6)
        def _():
            ring_first()

        @pl.when((n > 6) & (n % 3 == 0))
        def _():
            ring_hop(NZ // 2 - 1 - (n - 6) // 3)

        backward_window(REACH + 1 - 2 * s, h)
        backward_window(REACH - 2 * s, h)
        j = NZ // 2 + 1 - 2 * s - h // 2
        backward_prompt(j, 2 * (h % 2))
        backward_prompt(j, 2 * (h % 2) + 1)

        @pl.when(h % 2 == 1)
        def _():
            ring_odd(j)

        @pl.when(s == 1)
        def _():
            return_hop(REACH - 1, h)

    loop(KH * (REACH // 2), return_step)

    part = jnp.zeros((1, HD), F32)

    def query_back(raw, upstream):
        qhat, factor = rms(raw.astype(F32))
        u = upstream * g0
        inner = jnp.mean(u * qhat, axis=-1, keepdims=True)
        return factor * (u - qhat * inner), jnp.sum(upstream * qhat, axis=0, keepdims=True)

    def query_head(h):
        total = jnp.zeros((1, HD), F32)
        tail = dqt[h, :, RC:COLS].T * SCALE
        for g in range(SH):
            head = h * SH + g
            cols = slice(head * HD, (head + 1) * HD)
            upstream = dqt[h, :, g * RROWS : (g + 1) * RROWS].T * SCALE
            out, more = query_back(qr[:, cols], upstream)
            dqr[:, cols] = out.astype(BF)
            total = total + more
            out, more = query_back(qp[:, cols], tail[g * PROWS : (g + 1) * PROWS])
            dqp[:, cols] = out.astype(BF)
            total = total + more
        return total

    def gain_copy(i, j):
        return pltpu.make_async_remote_copy(
            src_ref=red.at[i], dst_ref=redr.at[i, j], send_sem=rds.at[i, j], recv_sem=rdr.at[i, j],
            device_id=partners[i][j], device_id_type=MESH,
        )

    steps = len(partners)

    def gain_start(i):
        if i < steps:
            for j in range(len(partners[i])):
                gain_copy(i, j).start()

    def gain_step(i):
        if i < steps:
            for j in range(len(partners[i])):
                gain_copy(i, j).wait_recv()
            total = red[i] + redr[i, 0]
            if len(partners[i]) == 3:
                total = total + (redr[i, 1] + redr[i, 2])
            red[i + 1] = total
            gain_start(i + 1)

    done = 0
    for s in range(REACH // 2 + 1, REACH):
        for h in range(KH):
            return_hop(REACH - s, h)
            n = KH * (s - 1) + h
            if n % 2 == 0 and n < NZ + 4:
                ring_cross(NZ // 2 - 1 - (n - 4) // 2)
            if n % 3 == 0 and n < KH * REACH - 5:
                ring_hop(NZ // 2 - 1 - (n - 6) // 3)
            if n == KH * REACH - 5:
                ring_last()
            if s == REACH // 2 + 1:
                part = part + query_head(h)
                if h == KH - 1:
                    red[0] = jnp.broadcast_to(part, (8, HD))
                    gain_start(0)
            elif h % 2 == 1:
                gain_step(done)
                done += 1
    def key_back(raw, upstream):
        khat, factor = rms(raw.astype(F32))
        u = upstream * g1
        inner = jnp.mean(u * khat, axis=-1, keepdims=True)
        return factor * (u - khat * inner)

    for h in range(KH):
        back_arrived(1, h)
    for h in range(KH):
        cols = slice(h * HD, (h + 1) * HD)
        vcols = slice((KH + h) * HD, (KH + h + 1) * HD)
        dkvp[:, cols] = key_back(kvp[:, cols], fin[h, :, 0:HD]).astype(BF)
        dkvp[:, vcols] = fin[h, :, HD : 2 * HD].astype(BF)
    for h in range(KH):
        cols = slice(h * HD, (h + 1) * HD)
        vcols = slice((KH + h) * HD, (KH + h + 1) * HD)
        own = ew[0, h, :, 0 : 2 * HD] + returned(0, h)
        dkvr[:, cols] = key_back(kvr[:, cols], own[:, 0:HD]).astype(BF)
        dkvr[:, vcols] = own[:, HD : 2 * HD].astype(BF)

    while done < steps:
        gain_step(done)
        done += 1
    scales = [(total_rows * heads) ** (-0.5) for heads in (KH * SH, KH)]
    whole = red[steps][0:1, :]
    ngrad[0:1, :] = whole * scales[0]
    ngrad[1:2, :] = whole * (g0 / g1) * scales[1]

    def sent(n):
        k = n // KH
        h = n % KH

        @pl.when(fwd_sends(h))
        def _():
            fwd(k, h).wait_send()

        @pl.when(back_sends(h))
        def _():
            back(k + 1, h).wait_send()

        @pl.when((h >= KH // 2) & (me == 0))
        def _():
            fwd_over(k, h).wait_send()

        @pl.when((h >= KH // 2) & (me == 2 * NZ - 1))
        def _():
            back_over(k + 1, h).wait_send()

    loop(KH * REACH, sent)

    def ring_sent(m):
        gather_two(m).wait_send()
        scatter_two(m + 1).wait_send()

    loop(NZ // 2 - 1, ring_sent)

    def half_sent(m):
        for copy in (gather_one, gather_y, gather_side, scatter_one, scatter_y, scatter_side):
            copy(m).wait_send()

    loop(NZ // 2, half_sent)
    for i in range(steps):
        for j in range(len(partners[i])):
            gain_copy(i, j).wait_send()


def per_device(mesh_shape, qp, qr, kvp, kvr, gp, gr, gains, lens):
    bits = [("resp", 1 << i) for i in range((mesh_shape["resp"] - 1).bit_length())]
    bits += [("prompt", 1 << i) for i in reversed(range((mesh_shape["prompt"] - 1).bit_length()))]
    rounds = tuple(tuple(bits[i : i + 2]) for i in range(0, len(bits), 2))
    total_rows = mesh_shape["prompt"] * mesh_shape["resp"] * (PROWS + RROWS)
    slots = len(rounds)
    vmem = pl.BlockSpec(memory_space=pltpu.VMEM)
    dma = pltpu.SemaphoreType.DMA
    block = (KH, RROWS, 2 * HD)
    pblock = (KH, PROWS, 2 * HD)
    scratch = [
        pltpu.VMEM((REACH + 1,) + block, BF),
        pltpu.VMEM((NZ, 2) + pblock, BF),
        pltpu.VMEM((REACH,) + block, BF),
        pltpu.VMEM((REACH,) + block, BF),
        pltpu.VMEM((NZ - 1,) + pblock, BF),
        pltpu.VMEM((NZ - 1,) + pblock, BF),
        pltpu.VMEM((NZ // 2,) + pblock, BF),
        pltpu.VMEM((NZ // 2,) + pblock, BF),
        pltpu.VMEM((NZ // 2,) + pblock, BF),
        pltpu.VMEM((NZ // 2,) + pblock, BF),
        pltpu.VMEM(pblock, F32),
        pltpu.VMEM((KH, COLS, HD), BF),
        pltpu.VMEM((KH, HD, COLS), BF),
        pltpu.VMEM((KH, COLS, HD), BF),
        pltpu.VMEM((KH, HD, COLS), BF),
        pltpu.VMEM((KH, HD, COLS), F32),
        pltpu.VMEM((REACH + 1, KH, RROWS, RC), F32),
        pltpu.VMEM((REACH + 1, KH, RROWS, RC), F32),
        pltpu.VMEM((NZ // 2, KH, 4 * PROWS, COLS), F32),
        pltpu.VMEM((NZ // 2, KH, 4 * PROWS, COLS), F32),
        pltpu.VMEM((KH, 1, COLS), F32),
        pltpu.VMEM((KH, 1, COLS), F32),
        pltpu.VMEM((KH, 1, COLS), F32),
        pltpu.VMEM((REACH + 1, KH, 1, RC), F32),
        pltpu.VMEM((NZ // 2, KH, 1, COLS), F32),
        pltpu.VMEM((slots + 1, 8, HD), F32),
        pltpu.VMEM((slots, 3, 8, HD), F32),
        dma((REACH, KH)), dma((REACH, KH)), dma((REACH, KH)),
        dma((REACH, KH)), dma((REACH, KH)), dma((REACH, KH)),
        dma((NZ,)), dma((NZ,)), dma((NZ,)), dma((NZ,)),
        dma((NZ,)), dma((NZ,)), dma((NZ // 2,)), dma((NZ // 2,)), dma((NZ // 2,)), dma((NZ // 2,)),
        dma((slots, 3)), dma((slots, 3)),
    ]
    width = qp.shape[2]
    kvwidth = kvp.shape[2]
    outs = pl.pallas_call(
        functools.partial(kernel, rounds, total_rows),
        out_shape=(
            jax.ShapeDtypeStruct((PROWS, width), BF),
            jax.ShapeDtypeStruct((RROWS, width), BF),
            jax.ShapeDtypeStruct((PROWS, kvwidth), BF),
            jax.ShapeDtypeStruct((RROWS, kvwidth), BF),
            jax.ShapeDtypeStruct((2, HD), F32),
        ),
        in_specs=[vmem] * 7 + [pl.BlockSpec(memory_space=pltpu.SMEM)],
        out_specs=(vmem,) * 5,
        scratch_shapes=scratch,
        compiler_params=pltpu.CompilerParams(
            collective_id=0, has_side_effects=True, vmem_limit_bytes=62 * 1024 * 1024
        ),
    )(qp[0], qr[0], kvp[0], kvr[0], gp[0], gr[0], gains, lens)
    return outs[0][None], outs[1][None], outs[2][None], outs[3][None], outs[4]


def solution(mesh):
    rows = P("prompt", "resp", None)
    return jax.shard_map(
        functools.partial(per_device, dict(mesh.shape)),
        mesh=mesh,
        in_specs=(rows,) * 6 + (P(), P("prompt", None)),
        out_specs=(rows,) * 4 + (P(),),
        check_vma=False,
    )
```

```python
import functools

import jax
import jax.numpy as jnp
from jax import lax
from jax.experimental import pallas as pl
from jax.experimental.pallas import tpu as pltpu
from jax.sharding import PartitionSpec as P

MESH = pl.DeviceIdType.MESH
KH = 4
SH = 4
HD = 128
EPS = 1e-06
SCALE = HD ** (-0.5)
LOG2E = 1.4426950408889634
RROWS = 128
PROWS = 32
REACH = 8
NZ = 16
RC = SH * RROWS
PC = SH * PROWS
COLS = RC + PC
MASKED = -1e30
BF = jnp.bfloat16
F32 = jnp.float32


def dot(a, b):
    return lax.dot_general(a, b, (((1,), (0,)), ((), ())), preferred_element_type=F32)


def rms(x):
    factor = lax.rsqrt(jnp.mean(x * x, axis=-1, keepdims=True) + EPS)
    return x * factor, factor


def flip(index, bit):
    return index + (1 - 2 * ((index // bit) % 2)) * bit


def kernel(
    rounds,
    total_rows,
    qp, qr, kvp, kvr, gp, gr, gains, lens,
    dqp, dqr, dkvp, dkvr, ngrad,
    win, relay, pg, retr, rets, zr, zs, yr, ys, sider, sides, fin,
    qn, qt, do, dt, dqt, ew, dw, ep, dp,
    mref, lref, aref, mw, mp, red, redr,
    fs, fr, fxs, fxr, bs, br, bxs, bxr, azs, azr, ays, ayr, rzs, rzr, rys, ryr, rxs, rxr, rds, rdr,
):
    me = lax.axis_index("resp")
    pr = lax.axis_index("prompt")
    y = me // NZ
    z = me % NZ
    nxt = (me + 1) % (2 * NZ)
    prv = (me + 2 * NZ - 1) % (2 * NZ)
    up1 = y * NZ + (z + 1) % NZ
    up2 = y * NZ + (z + 2) % NZ
    down1 = y * NZ + (z + NZ - 1) % NZ
    down2 = y * NZ + (z + NZ - 2) % NZ
    yp = (me + NZ) % (2 * NZ)

    def flipped(place, axis, bit):
        if axis == "prompt":
            return flip(place[0], bit), place[1]
        return place[0], flip(place[1], bit)

    partners = []
    for bits in rounds:
        places = [(pr, me)]
        for axis, bit in bits:
            places += [flipped(place, axis, bit) for place in places]
        partners.append(places[1:])
    friends = [(pr, i) for i in (nxt, prv, up1, up2, down1, down2, yp)]
    for places in partners:
        friends += places

    barrier = pltpu.get_barrier_semaphore()
    for friend in friends:
        pl.semaphore_signal(barrier, inc=1, device_id=friend, device_id_type=MESH)

    g0 = gains[0:1, :]
    g1 = gains[1:2, :]

    def remote(src, dst, ssem, rsem, resp):
        return pltpu.make_async_remote_copy(
            src_ref=src, dst_ref=dst, send_sem=ssem, recv_sem=rsem,
            device_id=(pr, resp), device_id_type=MESH,
        )

    first_device, last = me == 0, me == 2 * NZ - 1
    leaves, enters = me == NZ - 1, me == NZ
    half = KH // 2

    def fwd(k, h):
        return remote(win.at[k, h], win.at[k + 1, h], fs.at[k, h], fr.at[k, h], nxt)

    def fwd_corner(k, h):
        return remote(win.at[k, h], relay.at[k, h - half], fs.at[k, h], fxr.at[k, h], yp)

    def fwd_over(k, h):
        return remote(relay.at[k, h - half], win.at[k + 1, h], fxs.at[k, h], fr.at[k, h], up1)

    def back(k, h):
        i = k - 1
        return remote(rets.at[i, h], retr.at[i, h], bs.at[i, h], br.at[i, h], prv)

    def back_corner(k, h):
        i = k - 1
        return remote(rets.at[i, h], relay.at[i, h - half], bs.at[i, h], bxr.at[i, h], yp)

    def back_over(k, h):
        i = k - 1
        return remote(relay.at[i, h - half], retr.at[i, h], bxs.at[i, h], br.at[i, h], down1)

    def fwd_start(k, h):
        @pl.when((h >= half) & leaves)
        def _():
            fwd_corner(k, h).start()

        @pl.when(((h < half) | (me != NZ - 1)) & (me != 2 * NZ - 1))
        def _():
            fwd(k, h).start()

    def back_start(k, h):
        @pl.when((h >= half) & enters)
        def _():
            back_corner(k, h).start()

        @pl.when(((h < half) | (me != NZ)) & (me != 0))
        def _():
            back(k, h).start()

    def fwd_arrived(k, h):
        @pl.when((h >= half) & last)
        def _():
            fwd_corner(k, h).wait_recv()
            fwd_over(k, h).start()

        @pl.when(me != 0)
        def _():
            fwd(k, h).wait_recv()

    def back_arrived(k, h):
        @pl.when((h >= half) & first_device)
        def _():
            back_corner(k, h).wait_recv()
            back_over(k, h).start()

        @pl.when(me != 2 * NZ - 1)
        def _():
            back(k, h).wait_recv()

    def returned(k, h):
        return jnp.where(last, 0.0, retr[k, h].astype(F32))

    def gather_two(m):
        t = 2 * m
        return remote(pg.at[t, 0], pg.at[t + 2, 0], azs.at[t], azr.at[t], down2)

    def gather_one(m):
        t = 2 * m
        return remote(pg.at[t, 0], pg.at[t + 1, 0], azs.at[t + 1], azr.at[t + 1], down1)

    def gather_y(m):
        t = 2 * m
        return remote(pg.at[t, 0], pg.at[t, 1], ays.at[t], ayr.at[t], yp)

    def gather_side(m):
        t = 2 * m
        return remote(pg.at[t, 1], pg.at[t + 1, 1], ays.at[t + 1], ayr.at[t + 1], down1)

    def scatter_one(m):
        t = 2 * m
        return remote(zs.at[t], zr.at[t], rzs.at[t], rzr.at[t], up1)

    def scatter_two(m):
        t = 2 * m - 1
        return remote(zs.at[t], zr.at[t], rzs.at[t], rzr.at[t], up2)

    def scatter_side(m):
        return remote(sides.at[m], sider.at[m], rxs.at[m], rxr.at[m], up1)

    def scatter_y(m):
        return remote(ys.at[m], yr.at[m], rys.at[m], ryr.at[m], yp)

    @pl.when(first_device)
    def _():
        win[1:] = jnp.zeros((REACH, KH, RROWS, 2 * HD), BF)

    @pl.when(last)
    def _():
        retr[...] = jnp.zeros((REACH, KH, RROWS, 2 * HD), BF)

    for h in range(KH):
        cols = slice(h * HD, (h + 1) * HD)
        vcols = slice((KH + h) * HD, (KH + h + 1) * HD)
        khat, _ = rms(kvr[:, cols].astype(F32))
        win[0, h, :, 0:HD] = (khat * g1).astype(BF)
        win[0, h, :, HD : 2 * HD] = kvr[:, vcols]
        khat, _ = rms(kvp[:, cols].astype(F32))
        pg[0, 0, h, :, 0:HD] = (khat * g1).astype(BF)
        pg[0, 0, h, :, HD : 2 * HD] = kvp[:, vcols]

    pl.semaphore_wait(barrier, len(friends))
    gather_two(0).start()
    gather_one(0).start()
    gather_y(0).start()
    for h in range(KH):
        fwd_start(0, h)

    for h in range(KH):
        for g in range(SH):
            head = h * SH + g
            cols = slice(head * HD, (head + 1) * HD)
            rows = slice(g * RROWS, (g + 1) * RROWS)
            prows = slice(RC + g * PROWS, RC + (g + 1) * PROWS)
            qhat, _ = rms(qr[:, cols].astype(F32))
            low = (qhat * g0).astype(BF)
            qn[h, rows, :] = low
            qt[h, :, rows] = low.astype(F32).T.astype(BF)
            qhat, _ = rms(qp[:, cols].astype(F32))
            qn[h, prows, :] = (qhat * g0).astype(BF)
            do[h, rows, :] = gr[:, cols]
            dt[h, :, rows] = gr[:, cols].astype(F32).T.astype(BF)
            do[h, prows, :] = gp[:, cols]
        qt[h, :, RC:COLS] = qn[h, RC:COLS, :].astype(F32).T.astype(BF)
        dt[h, :, RC:COLS] = do[h, RC:COLS, :].astype(F32).T.astype(BF)
        dqt[h] = jnp.zeros((HD, COLS), F32)

    lane = lax.broadcasted_iota(jnp.int32, (1, RC), 1)
    row_index = me * RROWS + lane % RROWS
    first = jnp.zeros((1, RC), jnp.int32)
    end = jnp.int32(0)
    for j in range(lens.shape[1]):
        end = end + lens[0, j]
        first = jnp.where(row_index >= end, end, first)

    def online(keys, vals, h, lo, hi, allowed, eref, dref, mold, lold, aold):
        cols = slice(lo, hi)
        scores = dot(keys, qt[h, :, cols]) * (SCALE * LOG2E)
        probs_grad = dot(vals, dt[h, :, cols])
        if allowed is not None:
            scores = jnp.where(allowed, scores, MASKED)
        top = jnp.maximum(mold, jnp.max(scores, axis=0, keepdims=True))
        shrink = jnp.exp2(mold - top)
        expo = jnp.exp2(scores - top)
        mref[h, :, cols] = top
        lref[h, :, cols] = lold * shrink + jnp.sum(expo, axis=0, keepdims=True)
        aref[h, :, cols] = aold * shrink + jnp.sum(expo * probs_grad, axis=0, keepdims=True)
        eref[:, cols] = expo
        dref[:, cols] = probs_grad
        return top

    def old(h, lo, hi):
        return mref[h, :, lo:hi], lref[h, :, lo:hi], aref[h, :, lo:hi]

    def key_rows(k):
        return (me - k) * RROWS + lax.broadcasted_iota(jnp.int32, (RROWS, RC), 0)

    def window_keys(k, h):
        return win[k, h, :, 0:HD], win[k, h, :, HD : 2 * HD]

    def forward_own(h):
        keys, vals = window_keys(0, h)
        index = key_rows(0)
        allowed = (index >= first) & (index <= row_index)
        lowest = jnp.full((1, RC), MASKED, F32)
        zero = jnp.zeros((1, RC), F32)
        top = online(keys, vals, h, 0, RC, allowed, ew.at[0, h], dw.at[0, h], lowest, zero, zero)
        mw[0, h] = top
        mref[h, :, RC:COLS] = jnp.full((1, PC), MASKED, F32)
        lref[h, :, RC:COLS] = jnp.zeros((1, PC), F32)
        aref[h, :, RC:COLS] = jnp.zeros((1, PC), F32)

    def forward_window(k, h):
        keys, vals = window_keys(k, h)
        allowed = key_rows(k) >= first
        mw[k, h] = online(keys, vals, h, 0, RC, allowed, ew.at[k, h], dw.at[k, h], *old(h, 0, RC))

    def prompt_keys(j, h):
        keys = pg[pl.ds(2 * j, 2), :, h, :, 0:HD].reshape(4 * PROWS, HD)
        vals = pg[pl.ds(2 * j, 2), :, h, :, HD : 2 * HD].reshape(4 * PROWS, HD)
        return keys, vals

    def forward_prompt(j, h):
        keys, vals = prompt_keys(j, h)
        sub = lax.broadcasted_iota(jnp.int32, (4 * PROWS, PC), 0)
        ring = jnp.where((sub & 32) == 0, y, 1 - y)
        chip = (z + 2 * j + (sub >> 6)) & (NZ - 1)
        position = (ring * NZ + chip) * PROWS + (sub & 31)
        query = me * PROWS + (lax.broadcasted_iota(jnp.int32, (4 * PROWS, PC), 1) & 31)
        er, dr = ep.at[j, h], dp.at[j, h]
        mp[j, h, :, 0:RC] = online(keys, vals, h, 0, RC, None, er, dr, *old(h, 0, RC))
        mp[j, h, :, RC:COLS] = online(
            keys, vals, h, RC, COLS, position <= query, er, dr, *old(h, RC, COLS)
        )

    def loop(count, body):
        def step(i, carry):
            body(i)
            return carry

        lax.fori_loop(0, count, step, 0)

    loop(KH, forward_own)

    def forward_step(n):
        k = n // KH
        h = n % KH
        fwd_arrived(k, h)

        @pl.when(k < REACH - 1)
        def _():
            fwd_start(k + 1, h)

        @pl.when((n % 3 == 2) & (n < 3 * (NZ // 2)))
        def _():
            m = n // 3

            @pl.when(m < NZ // 2 - 1)
            def _():
                gather_two(m).wait_recv()

                @pl.when(m < NZ // 2 - 2)
                def _():
                    gather_two(m + 1).start()

                gather_one(m + 1).start()
                gather_y(m + 1).start()

            gather_y(m).wait_recv()
            gather_side(m).start()

        forward_window(k + 1, h)

        @pl.when(k >= 1)
        def _():
            @pl.when(h == 0)
            def _():
                gather_one(k - 1).wait_recv()
                gather_side(k - 1).wait_recv()

            forward_prompt(k - 1, h)

        @pl.when(k == REACH - 1)
        def _():
            @pl.when(h == 0)
            def _():
                gather_one(NZ // 2 - 1).wait_recv()
                gather_side(NZ // 2 - 1).wait_recv()

            forward_prompt(NZ // 2 - 1, h)

    loop(KH * REACH, forward_step)

    def finish(h):
        inverse = 1.0 / lref[h]
        lref[h] = inverse
        aref[h] = aref[h] * inverse

    loop(KH, finish)

    def backward(keys, h, hi, top, eref, dref):
        weight = jnp.exp2(top - mref[h, :, 0:hi]) * lref[h, :, 0:hi]
        probs = eref[:, 0:hi] * weight
        low = probs.astype(BF)
        ds = (probs * (dref[:, 0:hi] - aref[h, :, 0:hi])).astype(BF)
        dk = dot(ds, qn[h, 0:hi, :]) * SCALE
        dv = dot(low, do[h, 0:hi, :])
        dqt[h, :, 0:hi] += dot(keys.astype(F32).T.astype(BF), ds)
        return dk, dv

    def backward_window(k, h):
        dk, dv = backward(window_keys(k, h)[0], h, RC, mw[k, h], ew.at[k, h], dw.at[k, h])
        ew[k, h, :, 0:HD] = dk
        ew[k, h, :, HD : 2 * HD] = dv

    def backward_prompt(j, h):
        dk, dv = backward(prompt_keys(j, h)[0], h, COLS, mp[j, h], ep.at[j, h], dp.at[j, h])
        ep[j, h, :, 0:HD] = dk
        ep[j, h, :, HD : 2 * HD] = dv
        sides[j, h, :, 0:HD] = dk[3 * PROWS :].astype(BF)
        sides[j, h, :, HD : 2 * HD] = dv[3 * PROWS :].astype(BF)

    def return_first(h):
        backward_window(REACH, h)
        rets[REACH - 1, h] = ew[REACH, h, :, 0 : 2 * HD].astype(BF)
        back_start(REACH, h)

    loop(KH, return_first)

    def return_hop(k, h):
        back_arrived(k + 1, h)
        rets[k - 1, h] = (ew[k, h, :, 0 : 2 * HD] + returned(k, h)).astype(BF)
        back_start(k, h)

    def prompt_part(j, quarter):
        return ep[j, :, quarter * PROWS : (quarter + 1) * PROWS, 0 : 2 * HD]

    def ring_odd(m):
        zs[2 * m] = prompt_part(m, 2).astype(BF)
        scatter_one(m).start()
        scatter_side(m).start()

    def ring_cross(m):
        scatter_side(m).wait_recv()
        ys[m] = (prompt_part(m, 1) + sider[m].astype(F32)).astype(BF)
        scatter_y(m).start()

    def ring_even(m):
        scatter_y(m).wait_recv()
        scatter_one(m).wait_recv()
        return prompt_part(m, 0) + yr[m].astype(F32) + zr[2 * m].astype(F32)

    def ring_first():
        m = NZ // 2 - 1
        zs[2 * m - 1] = ring_even(m).astype(BF)
        scatter_two(m).start()

    def ring_hop(m):
        total = ring_even(m)
        scatter_two(m + 1).wait_recv()
        zs[2 * m - 1] = (total + zr[2 * m + 1].astype(F32)).astype(BF)
        scatter_two(m).start()

    def ring_last():
        total = ring_even(0)
        scatter_two(1).wait_recv()
        fin[...] = total + zr[1].astype(F32)

    def return_step(n):
        s = 1 + n // KH
        h = n % KH

        @pl.when(s > 1)
        def _():
            return_hop(REACH - s, h)

        @pl.when((n >= 4) & (n % 2 == 0))
        def _():
            ring_cross(NZ // 2 - 1 - (n - 4) // 2)

        @pl.when(n == 6)
        def _():
            ring_first()

        @pl.when((n > 6) & (n % 3 == 0))
        def _():
            ring_hop(NZ // 2 - 1 - (n - 6) // 3)

        backward_window(REACH + 1 - 2 * s, h)
        backward_window(REACH - 2 * s, h)
        j = NZ // 2 + 1 - 2 * s - h // 2
        backward_prompt(j, 2 * (h % 2))
        backward_prompt(j, 2 * (h % 2) + 1)

        @pl.when(h % 2 == 1)
        def _():
            ring_odd(j)

        @pl.when(s == 1)
        def _():
            return_hop(REACH - 1, h)

    loop(KH * (REACH // 2), return_step)

    part = jnp.zeros((1, HD), F32)

    def query_back(raw, upstream):
        qhat, factor = rms(raw.astype(F32))
        u = upstream * g0
        inner = jnp.mean(u * qhat, axis=-1, keepdims=True)
        return factor * (u - qhat * inner), jnp.sum(upstream * qhat, axis=0, keepdims=True)

    def query_head(h):
        total = jnp.zeros((1, HD), F32)
        tail = dqt[h, :, RC:COLS].T * SCALE
        for g in range(SH):
            head = h * SH + g
            cols = slice(head * HD, (head + 1) * HD)
            upstream = dqt[h, :, g * RROWS : (g + 1) * RROWS].T * SCALE
            out, more = query_back(qr[:, cols], upstream)
            dqr[:, cols] = out.astype(BF)
            total = total + more
            out, more = query_back(qp[:, cols], tail[g * PROWS : (g + 1) * PROWS])
            dqp[:, cols] = out.astype(BF)
            total = total + more
        return total

    def gain_copy(i, j):
        return pltpu.make_async_remote_copy(
            src_ref=red.at[i], dst_ref=redr.at[i, j], send_sem=rds.at[i, j], recv_sem=rdr.at[i, j],
            device_id=partners[i][j], device_id_type=MESH,
        )

    steps = len(partners)

    def gain_start(i):
        if i < steps:
            for j in range(len(partners[i])):
                gain_copy(i, j).start()

    def gain_step(i):
        if i < steps:
            for j in range(len(partners[i])):
                gain_copy(i, j).wait_recv()
            parts = [red[i]] + [redr[i, j] for j in range(len(partners[i]))]
            while len(parts) > 1:
                parts = [parts[j] + parts[j + 1] for j in range(0, len(parts), 2)]
            red[i + 1] = parts[0]
            gain_start(i + 1)

    for h in range(KH):
        part = part + query_head(h)
    red[0] = jnp.broadcast_to(part, (8, HD))
    gain_start(0)
    done = 0
    for s in range(REACH // 2 + 1, REACH):
        for h in range(KH):
            return_hop(REACH - s, h)
            n = KH * (s - 1) + h
            if n % 2 == 0 and n < NZ + 4:
                ring_cross(NZ // 2 - 1 - (n - 4) // 2)
            if n % 3 == 0 and n < KH * REACH - 5:
                ring_hop(NZ // 2 - 1 - (n - 6) // 3)
            if n == KH * REACH - 5:
                ring_last()
            if (s, h) in ((REACH - 2, 0), (REACH - 1, 0), (REACH - 1, KH - 1)):
                gain_step(done)
                done += 1
    def key_back(raw, upstream):
        khat, factor = rms(raw.astype(F32))
        u = upstream * g1
        inner = jnp.mean(u * khat, axis=-1, keepdims=True)
        return factor * (u - khat * inner)

    for h in range(KH):
        back_arrived(1, h)
    for h in range(KH):
        cols = slice(h * HD, (h + 1) * HD)
        vcols = slice((KH + h) * HD, (KH + h + 1) * HD)
        dkvp[:, cols] = key_back(kvp[:, cols], fin[h, :, 0:HD]).astype(BF)
        dkvp[:, vcols] = fin[h, :, HD : 2 * HD].astype(BF)
    for h in range(KH):
        cols = slice(h * HD, (h + 1) * HD)
        vcols = slice((KH + h) * HD, (KH + h + 1) * HD)
        own = ew[0, h, :, 0 : 2 * HD] + returned(0, h)
        dkvr[:, cols] = key_back(kvr[:, cols], own[:, 0:HD]).astype(BF)
        dkvr[:, vcols] = own[:, HD : 2 * HD].astype(BF)

    while done < steps:
        gain_step(done)
        done += 1
    scales = [(total_rows * heads) ** (-0.5) for heads in (KH * SH, KH)]
    whole = red[steps][0:1, :]
    ngrad[0:1, :] = whole * scales[0]
    ngrad[1:2, :] = whole * (g0 / g1) * scales[1]

    def sent(n):
        k = n // KH
        h = n % KH

        @pl.when(me != 2 * NZ - 1)
        def _():
            fwd(k, h).wait_send()

        @pl.when(me != 0)
        def _():
            back(k + 1, h).wait_send()

        @pl.when((h >= half) & last)
        def _():
            fwd_over(k, h).wait_send()

        @pl.when((h >= half) & first_device)
        def _():
            back_over(k + 1, h).wait_send()

    loop(KH * REACH, sent)

    def ring_sent(m):
        gather_two(m).wait_send()
        scatter_two(m + 1).wait_send()

    loop(NZ // 2 - 1, ring_sent)

    def half_sent(m):
        for copy in (gather_one, gather_y, gather_side, scatter_one, scatter_y, scatter_side):
            copy(m).wait_send()

    loop(NZ // 2, half_sent)
    for i in range(steps):
        for j in range(len(partners[i])):
            gain_copy(i, j).wait_send()


def copy_out(*refs):
    for source, target in zip(refs[:5], refs[5:]):
        target[...] = source[...]


def per_device(mesh_shape, qp, qr, kvp, kvr, gp, gr, gains, lens):
    bits = [("resp", 1 << i) for i in range((mesh_shape["resp"] - 1).bit_length())]
    bits += [("prompt", 1 << i) for i in reversed(range((mesh_shape["prompt"] - 1).bit_length()))]
    rounds = tuple(tuple(bits[i : i + 3]) for i in range(0, len(bits), 3))
    total_rows = mesh_shape["prompt"] * mesh_shape["resp"] * (PROWS + RROWS)
    slots = len(rounds)
    vmem = pl.BlockSpec(memory_space=pltpu.VMEM)
    dma = pltpu.SemaphoreType.DMA
    block = (KH, RROWS, 2 * HD)
    pblock = (KH, PROWS, 2 * HD)
    scratch = [
        pltpu.VMEM((REACH + 1,) + block, BF),
        pltpu.VMEM((REACH, KH // 2, RROWS, 2 * HD), BF),
        pltpu.VMEM((NZ, 2) + pblock, BF),
        pltpu.VMEM((REACH,) + block, BF),
        pltpu.VMEM((REACH,) + block, BF),
        pltpu.VMEM((NZ - 1,) + pblock, BF),
        pltpu.VMEM((NZ - 1,) + pblock, BF),
        pltpu.VMEM((NZ // 2,) + pblock, BF),
        pltpu.VMEM((NZ // 2,) + pblock, BF),
        pltpu.VMEM((NZ // 2,) + pblock, BF),
        pltpu.VMEM((NZ // 2,) + pblock, BF),
        pltpu.VMEM(pblock, F32),
        pltpu.VMEM((KH, COLS, HD), BF),
        pltpu.VMEM((KH, HD, COLS), BF),
        pltpu.VMEM((KH, COLS, HD), BF),
        pltpu.VMEM((KH, HD, COLS), BF),
        pltpu.VMEM((KH, HD, COLS), F32),
        pltpu.VMEM((REACH + 1, KH, RROWS, RC), F32),
        pltpu.VMEM((REACH + 1, KH, RROWS, RC), F32),
        pltpu.VMEM((NZ // 2, KH, 4 * PROWS, COLS), F32),
        pltpu.VMEM((NZ // 2, KH, 4 * PROWS, COLS), F32),
        pltpu.VMEM((KH, 1, COLS), F32),
        pltpu.VMEM((KH, 1, COLS), F32),
        pltpu.VMEM((KH, 1, COLS), F32),
        pltpu.VMEM((REACH + 1, KH, 1, RC), F32),
        pltpu.VMEM((NZ // 2, KH, 1, COLS), F32),
        pltpu.VMEM((slots + 1, 8, HD), F32),
        pltpu.VMEM((slots, 7, 8, HD), F32),
        dma((REACH, KH)), dma((REACH, KH)), dma((REACH, KH)), dma((REACH, KH)),
        dma((REACH, KH)), dma((REACH, KH)), dma((REACH, KH)), dma((REACH, KH)),
        dma((NZ,)), dma((NZ,)), dma((NZ,)), dma((NZ,)),
        dma((NZ,)), dma((NZ,)), dma((NZ // 2,)), dma((NZ // 2,)), dma((NZ // 2,)), dma((NZ // 2,)),
        dma((slots, 7)), dma((slots, 7)),
    ]
    width = qp.shape[2]
    kvwidth = kvp.shape[2]
    outs = pl.pallas_call(
        functools.partial(kernel, rounds, total_rows),
        out_shape=(
            jax.ShapeDtypeStruct((PROWS, width), BF),
            jax.ShapeDtypeStruct((RROWS, width), BF),
            jax.ShapeDtypeStruct((PROWS, kvwidth), BF),
            jax.ShapeDtypeStruct((RROWS, kvwidth), BF),
            jax.ShapeDtypeStruct((2, HD), F32),
        ),
        in_specs=[vmem] * 7 + [pl.BlockSpec(memory_space=pltpu.SMEM)],
        out_specs=(vmem,) * 5,
        scratch_shapes=scratch,
        compiler_params=pltpu.CompilerParams(
            collective_id=0, has_side_effects=True, vmem_limit_bytes=62 * 1024 * 1024
        ),
    )(qp[0], qr[0], kvp[0], kvr[0], gp[0], gr[0], gains, lens)
    outs = pl.pallas_call(
        copy_out,
        out_shape=tuple(jax.ShapeDtypeStruct(out.shape, out.dtype) for out in outs),
        in_specs=[vmem] * 5,
        out_specs=(vmem,) * 5,
    )(*outs)
    return outs[0][None], outs[1][None], outs[2][None], outs[3][None], outs[4]


def solution(mesh):
    rows = P("prompt", "resp", None)
    return jax.shard_map(
        functools.partial(per_device, dict(mesh.shape)),
        mesh=mesh,
        in_specs=(rows,) * 6 + (P(), P("prompt", None)),
        out_specs=(rows,) * 4 + (P(),),
        check_vma=False,
    )
```

```python
import functools

import jax
import jax.numpy as jnp
from jax import lax
from jax.experimental import pallas as pl
from jax.experimental.pallas import tpu as pltpu
from jax.sharding import PartitionSpec as P

MESH = pl.DeviceIdType.MESH
KH = 4
SH = 4
HD = 128
EPS = 1e-06
SCALE = HD ** (-0.5)
LOG2E = 1.4426950408889634
RROWS = 128
PROWS = 32
REACH = 8
NZ = 16
RC = SH * RROWS
PC = SH * PROWS
COLS = RC + PC
MASKED = -1e30
BF = jnp.bfloat16
F32 = jnp.float32


def dot(a, b):
    return lax.dot_general(a, b, (((1,), (0,)), ((), ())), preferred_element_type=F32)


def rms(x):
    factor = lax.rsqrt(jnp.mean(x * x, axis=-1, keepdims=True) + EPS)
    return x * factor, factor


def flip(index, bit):
    return index + (1 - 2 * ((index // bit) % 2)) * bit


def kernel(
    rounds,
    total_rows,
    qp, qr, kvp, kvr, gp, gr, gains, lens,
    dqp, dqr, dkvp, dkvr, ngrad,
    win, relay, pg, retr, rets, zr, zs, yr, ys, sider, sides, fin,
    qn, qt, do, dt, dqt, ew, dw, ep, dp,
    mref, lref, aref, mw, mp, red, redr,
    fs, fr, fxs, fxr, bs, br, bxs, bxr, azs, azr, ays, ayr, rzs, rzr, rys, ryr, rxs, rxr, rds, rdr,
):
    me = lax.axis_index("resp")
    pr = lax.axis_index("prompt")
    y = me // NZ
    z = me % NZ
    nxt = (me + 1) % (2 * NZ)
    prv = (me + 2 * NZ - 1) % (2 * NZ)
    up1 = y * NZ + (z + 1) % NZ
    up2 = y * NZ + (z + 2) % NZ
    down1 = y * NZ + (z + NZ - 1) % NZ
    down2 = y * NZ + (z + NZ - 2) % NZ
    yp = (me + NZ) % (2 * NZ)

    def flipped(place, axis, bit):
        if axis == "prompt":
            return flip(place[0], bit), place[1]
        return place[0], flip(place[1], bit)

    partners = []
    for bits in rounds:
        places = [(pr, me)]
        for axis, bit in bits:
            places += [flipped(place, axis, bit) for place in places]
        partners.append(places[1:])
    friends = [(pr, i) for i in (nxt, prv, up1, up2, down1, down2, yp)]
    for places in partners:
        friends += places

    barrier = pltpu.get_barrier_semaphore()
    for friend in friends:
        pl.semaphore_signal(barrier, inc=1, device_id=friend, device_id_type=MESH)

    g0 = gains[0:1, :]
    g1 = gains[1:2, :]

    def remote(src, dst, ssem, rsem, resp):
        return pltpu.make_async_remote_copy(
            src_ref=src, dst_ref=dst, send_sem=ssem, recv_sem=rsem,
            device_id=(pr, resp), device_id_type=MESH,
        )

    first_device, last = me == 0, me == 2 * NZ - 1
    leaves, enters = me == NZ - 1, me == NZ
    half = KH // 2

    def fwd(k, h):
        return remote(win.at[k, h], win.at[k + 1, h], fs.at[k, h], fr.at[k, h], nxt)

    def fwd_corner(k, h):
        return remote(win.at[k, h], relay.at[k, h - half], fs.at[k, h], fxr.at[k, h], yp)

    def fwd_over(k, h):
        return remote(relay.at[k, h - half], win.at[k + 1, h], fxs.at[k, h], fr.at[k, h], up1)

    def back(k, h):
        i = k - 1
        return remote(rets.at[i, h], retr.at[i, h], bs.at[i, h], br.at[i, h], prv)

    def back_corner(k, h):
        i = k - 1
        return remote(rets.at[i, h], relay.at[i, h - half], bs.at[i, h], bxr.at[i, h], yp)

    def back_over(k, h):
        i = k - 1
        return remote(relay.at[i, h - half], retr.at[i, h], bxs.at[i, h], br.at[i, h], down1)

    def fwd_start(k, h):
        @pl.when((h >= half) & leaves)
        def _():
            fwd_corner(k, h).start()

        @pl.when(((h < half) | (me != NZ - 1)) & (me != 2 * NZ - 1))
        def _():
            fwd(k, h).start()

    def back_start(k, h):
        @pl.when((h >= half) & enters)
        def _():
            back_corner(k, h).start()

        @pl.when(((h < half) | (me != NZ)) & (me != 0))
        def _():
            back(k, h).start()

    def fwd_arrived(k, h):
        @pl.when((h >= half) & last)
        def _():
            fwd_corner(k, h).wait_recv()
            fwd_over(k, h).start()

        @pl.when(me != 0)
        def _():
            fwd(k, h).wait_recv()

    def back_arrived(k, h):
        @pl.when((h >= half) & first_device)
        def _():
            back_corner(k, h).wait_recv()
            back_over(k, h).start()

        @pl.when(me != 2 * NZ - 1)
        def _():
            back(k, h).wait_recv()

    def returned(k, h):
        return jnp.where(last, 0.0, retr[k, h].astype(F32))

    def gather_two(m):
        t = 2 * m
        return remote(pg.at[t, 0], pg.at[t + 2, 0], azs.at[t], azr.at[t], down2)

    def gather_one(m):
        t = 2 * m
        return remote(pg.at[t, 0], pg.at[t + 1, 0], azs.at[t + 1], azr.at[t + 1], down1)

    def gather_y(m):
        t = 2 * m
        return remote(pg.at[t, 0], pg.at[t, 1], ays.at[t], ayr.at[t], yp)

    def gather_side(m):
        t = 2 * m
        return remote(pg.at[t, 1], pg.at[t + 1, 1], ays.at[t + 1], ayr.at[t + 1], down1)

    def scatter_one(m):
        t = 2 * m
        return remote(zs.at[t], zr.at[t], rzs.at[t], rzr.at[t], up1)

    def scatter_two(m):
        t = 2 * m - 1
        return remote(zs.at[t], zr.at[t], rzs.at[t], rzr.at[t], up2)

    def scatter_side(m):
        return remote(sides.at[m], sider.at[m], rxs.at[m], rxr.at[m], up1)

    def scatter_y(m):
        return remote(ys.at[m], yr.at[m], rys.at[m], ryr.at[m], yp)

    @pl.when(first_device)
    def _():
        win[1:] = jnp.zeros((REACH, KH, RROWS, 2 * HD), BF)

    @pl.when(last)
    def _():
        retr[...] = jnp.zeros((REACH, KH, RROWS, 2 * HD), BF)

    for h in range(KH):
        cols = slice(h * HD, (h + 1) * HD)
        vcols = slice((KH + h) * HD, (KH + h + 1) * HD)
        khat, _ = rms(kvr[:, cols].astype(F32))
        win[0, h, :, 0:HD] = (khat * g1).astype(BF)
        win[0, h, :, HD : 2 * HD] = kvr[:, vcols]
        khat, _ = rms(kvp[:, cols].astype(F32))
        pg[0, 0, h, :, 0:HD] = (khat * g1).astype(BF)
        pg[0, 0, h, :, HD : 2 * HD] = kvp[:, vcols]

    pl.semaphore_wait(barrier, len(friends))
    gather_two(0).start()
    gather_one(0).start()
    gather_y(0).start()
    for h in range(KH):
        fwd_start(0, h)

    for h in range(KH):
        for g in range(SH):
            head = h * SH + g
            cols = slice(head * HD, (head + 1) * HD)
            rows = slice(g * RROWS, (g + 1) * RROWS)
            prows = slice(RC + g * PROWS, RC + (g + 1) * PROWS)
            qhat, _ = rms(qr[:, cols].astype(F32))
            low = (qhat * g0).astype(BF)
            qn[h, rows, :] = low
            qt[h, :, rows] = low.astype(F32).T.astype(BF)
            qhat, _ = rms(qp[:, cols].astype(F32))
            qn[h, prows, :] = (qhat * g0).astype(BF)
            do[h, rows, :] = gr[:, cols]
            dt[h, :, rows] = gr[:, cols].astype(F32).T.astype(BF)
            do[h, prows, :] = gp[:, cols]
        qt[h, :, RC:COLS] = qn[h, RC:COLS, :].astype(F32).T.astype(BF)
        dt[h, :, RC:COLS] = do[h, RC:COLS, :].astype(F32).T.astype(BF)
        dqt[h] = jnp.zeros((HD, COLS), F32)

    lane = lax.broadcasted_iota(jnp.int32, (1, RC), 1)
    row_index = me * RROWS + lane % RROWS
    first = jnp.zeros((1, RC), jnp.int32)
    end = jnp.int32(0)
    for j in range(lens.shape[1]):
        end = end + lens[0, j]
        first = jnp.where(row_index >= end, end, first)

    def online(keys, vals, h, lo, hi, allowed, eref, dref, mold, lold, aold):
        cols = slice(lo, hi)
        scores = dot(keys, qt[h, :, cols]) * (SCALE * LOG2E)
        probs_grad = dot(vals, dt[h, :, cols])
        if allowed is not None:
            scores = jnp.where(allowed, scores, MASKED)
        top = jnp.maximum(mold, jnp.max(scores, axis=0, keepdims=True))
        shrink = jnp.exp2(mold - top)
        expo = jnp.exp2(scores - top)
        mref[h, :, cols] = top
        lref[h, :, cols] = lold * shrink + jnp.sum(expo, axis=0, keepdims=True)
        aref[h, :, cols] = aold * shrink + jnp.sum(expo * probs_grad, axis=0, keepdims=True)
        eref[:, cols] = expo
        dref[:, cols] = probs_grad
        return top

    def old(h, lo, hi):
        return mref[h, :, lo:hi], lref[h, :, lo:hi], aref[h, :, lo:hi]

    def key_rows(k):
        return (me - k) * RROWS + lax.broadcasted_iota(jnp.int32, (RROWS, RC), 0)

    def window_keys(k, h):
        return win[k, h, :, 0:HD], win[k, h, :, HD : 2 * HD]

    def forward_own(h):
        keys, vals = window_keys(0, h)
        index = key_rows(0)
        allowed = (index >= first) & (index <= row_index)
        lowest = jnp.full((1, RC), MASKED, F32)
        zero = jnp.zeros((1, RC), F32)
        top = online(keys, vals, h, 0, RC, allowed, ew.at[0, h], dw.at[0, h], lowest, zero, zero)
        mw[0, h] = top
        mref[h, :, RC:COLS] = jnp.full((1, PC), MASKED, F32)
        lref[h, :, RC:COLS] = jnp.zeros((1, PC), F32)
        aref[h, :, RC:COLS] = jnp.zeros((1, PC), F32)

    def forward_window(k, h):
        keys, vals = window_keys(k, h)
        allowed = key_rows(k) >= first
        mw[k, h] = online(keys, vals, h, 0, RC, allowed, ew.at[k, h], dw.at[k, h], *old(h, 0, RC))

    def prompt_keys(j, h):
        keys = pg[pl.ds(2 * j, 2), :, h, :, 0:HD].reshape(4 * PROWS, HD)
        vals = pg[pl.ds(2 * j, 2), :, h, :, HD : 2 * HD].reshape(4 * PROWS, HD)
        return keys, vals

    def forward_prompt(j, h):
        keys, vals = prompt_keys(j, h)
        sub = lax.broadcasted_iota(jnp.int32, (4 * PROWS, PC), 0)
        ring = jnp.where((sub & 32) == 0, y, 1 - y)
        chip = (z + 2 * j + (sub >> 6)) & (NZ - 1)
        position = (ring * NZ + chip) * PROWS + (sub & 31)
        query = me * PROWS + (lax.broadcasted_iota(jnp.int32, (4 * PROWS, PC), 1) & 31)
        er, dr = ep.at[j, h], dp.at[j, h]
        mp[j, h, :, 0:RC] = online(keys, vals, h, 0, RC, None, er, dr, *old(h, 0, RC))
        mp[j, h, :, RC:COLS] = online(
            keys, vals, h, RC, COLS, position <= query, er, dr, *old(h, RC, COLS)
        )

    def loop(count, body):
        def step(i, carry):
            body(i)
            return carry

        lax.fori_loop(0, count, step, 0)

    loop(KH, forward_own)

    def forward_step(n):
        k = n // KH
        h = n % KH
        fwd_arrived(k, h)

        @pl.when(k < REACH - 1)
        def _():
            fwd_start(k + 1, h)

        @pl.when((n % 3 == 2) & (n < 3 * (NZ // 2)))
        def _():
            m = n // 3

            @pl.when(m < NZ // 2 - 1)
            def _():
                gather_two(m).wait_recv()

                @pl.when(m < NZ // 2 - 2)
                def _():
                    gather_two(m + 1).start()

                gather_one(m + 1).start()
                gather_y(m + 1).start()

            gather_y(m).wait_recv()
            gather_side(m).start()

        forward_window(k + 1, h)

        @pl.when(k >= 1)
        def _():
            @pl.when(h == 0)
            def _():
                gather_one(k - 1).wait_recv()
                gather_side(k - 1).wait_recv()

            forward_prompt(k - 1, h)

        @pl.when(k == REACH - 1)
        def _():
            @pl.when(h == 0)
            def _():
                gather_one(NZ // 2 - 1).wait_recv()
                gather_side(NZ // 2 - 1).wait_recv()

            forward_prompt(NZ // 2 - 1, h)

    loop(KH * REACH, forward_step)

    def finish(h):
        inverse = 1.0 / lref[h]
        lref[h] = inverse
        aref[h] = aref[h] * inverse

    loop(KH, finish)

    def backward(keys, h, hi, top, eref, dref):
        weight = jnp.exp2(top - mref[h, :, 0:hi]) * lref[h, :, 0:hi]
        probs = eref[:, 0:hi] * weight
        low = probs.astype(BF)
        ds = (probs * (dref[:, 0:hi] - aref[h, :, 0:hi])).astype(BF)
        dk = dot(ds, qn[h, 0:hi, :]) * SCALE
        dv = dot(low, do[h, 0:hi, :])
        dqt[h, :, 0:hi] += dot(keys.astype(F32).T.astype(BF), ds)
        return dk, dv

    def backward_window(k, h):
        dk, dv = backward(window_keys(k, h)[0], h, RC, mw[k, h], ew.at[k, h], dw.at[k, h])
        ew[k, h, :, 0:HD] = dk
        ew[k, h, :, HD : 2 * HD] = dv

    def backward_prompt(j, h):
        dk, dv = backward(prompt_keys(j, h)[0], h, COLS, mp[j, h], ep.at[j, h], dp.at[j, h])
        ep[j, h, :, 0:HD] = dk
        ep[j, h, :, HD : 2 * HD] = dv
        sides[j, h, :, 0:HD] = dk[3 * PROWS :].astype(BF)
        sides[j, h, :, HD : 2 * HD] = dv[3 * PROWS :].astype(BF)

    def return_first(h):
        backward_window(REACH, h)
        rets[REACH - 1, h] = ew[REACH, h, :, 0 : 2 * HD].astype(BF)
        back_start(REACH, h)

    loop(KH, return_first)

    def return_hop(k, h):
        back_arrived(k + 1, h)
        rets[k - 1, h] = (ew[k, h, :, 0 : 2 * HD] + returned(k, h)).astype(BF)
        back_start(k, h)

    def prompt_part(j, quarter):
        return ep[j, :, quarter * PROWS : (quarter + 1) * PROWS, 0 : 2 * HD]

    def ring_odd(m):
        zs[2 * m] = prompt_part(m, 2).astype(BF)
        scatter_one(m).start()
        scatter_side(m).start()

    def ring_cross(m):
        scatter_side(m).wait_recv()
        ys[m] = (prompt_part(m, 1) + sider[m].astype(F32)).astype(BF)
        scatter_y(m).start()

    def ring_even(m):
        scatter_y(m).wait_recv()
        scatter_one(m).wait_recv()
        return prompt_part(m, 0) + yr[m].astype(F32) + zr[2 * m].astype(F32)

    def ring_first():
        m = NZ // 2 - 1
        zs[2 * m - 1] = ring_even(m).astype(BF)
        scatter_two(m).start()

    def ring_hop(m):
        total = ring_even(m)
        scatter_two(m + 1).wait_recv()
        zs[2 * m - 1] = (total + zr[2 * m + 1].astype(F32)).astype(BF)
        scatter_two(m).start()

    def ring_last():
        total = ring_even(0)
        scatter_two(1).wait_recv()
        fin[...] = total + zr[1].astype(F32)

    def return_step(n):
        s = 1 + n // KH
        h = n % KH

        @pl.when(s > 1)
        def _():
            return_hop(REACH - s, h)

        @pl.when((n >= 4) & (n % 2 == 0))
        def _():
            ring_cross(NZ // 2 - 1 - (n - 4) // 2)

        @pl.when(n == 6)
        def _():
            ring_first()

        @pl.when((n > 6) & (n % 3 == 0))
        def _():
            ring_hop(NZ // 2 - 1 - (n - 6) // 3)

        backward_window(REACH + 1 - 2 * s, h)
        backward_window(REACH - 2 * s, h)
        j = NZ // 2 + 1 - 2 * s - h // 2
        backward_prompt(j, 2 * (h % 2))
        backward_prompt(j, 2 * (h % 2) + 1)

        @pl.when(h % 2 == 1)
        def _():
            ring_odd(j)

        @pl.when(s == 1)
        def _():
            return_hop(REACH - 1, h)

    loop(KH * (REACH // 2), return_step)

    part = jnp.zeros((1, HD), F32)

    def query_back(raw, upstream):
        qhat, factor = rms(raw.astype(F32))
        u = upstream * g0
        inner = jnp.mean(u * qhat, axis=-1, keepdims=True)
        return factor * (u - qhat * inner), jnp.sum(upstream * qhat, axis=0, keepdims=True)

    def query_head(h):
        total = jnp.zeros((1, HD), F32)
        tail = dqt[h, :, RC:COLS].T * SCALE
        for g in range(SH):
            head = h * SH + g
            cols = slice(head * HD, (head + 1) * HD)
            upstream = dqt[h, :, g * RROWS : (g + 1) * RROWS].T * SCALE
            out, more = query_back(qr[:, cols], upstream)
            dqr[:, cols] = out.astype(BF)
            total = total + more
            out, more = query_back(qp[:, cols], tail[g * PROWS : (g + 1) * PROWS])
            dqp[:, cols] = out.astype(BF)
            total = total + more
        return total

    def gain_copy(i, j):
        return pltpu.make_async_remote_copy(
            src_ref=red.at[i], dst_ref=redr.at[i, j], send_sem=rds.at[i, j], recv_sem=rdr.at[i, j],
            device_id=partners[i][j], device_id_type=MESH,
        )

    steps = len(partners)

    def gain_start(i):
        if i < steps:
            for j in range(len(partners[i])):
                gain_copy(i, j).start()

    def gain_step(i):
        if i < steps:
            for j in range(len(partners[i])):
                gain_copy(i, j).wait_recv()
            parts = [red[i]] + [redr[i, j] for j in range(len(partners[i]))]
            while len(parts) > 1:
                parts = [parts[j] + parts[j + 1] for j in range(0, len(parts), 2)]
            red[i + 1] = parts[0]
            gain_start(i + 1)

    for h in range(KH):
        part = part + query_head(h)
    red[0] = jnp.broadcast_to(part, (8, HD))
    gain_start(0)
    done = 0
    for s in range(REACH // 2 + 1, REACH):
        for h in range(KH):
            return_hop(REACH - s, h)
            n = KH * (s - 1) + h
            if n % 2 == 0 and n < NZ + 4:
                ring_cross(NZ // 2 - 1 - (n - 4) // 2)
            if n % 3 == 0 and n < KH * REACH - 5:
                ring_hop(NZ // 2 - 1 - (n - 6) // 3)
            if n == KH * REACH - 5:
                ring_last()
            if (s, h) in ((REACH - 2, KH - 1), (REACH - 1, KH - 1)):
                gain_step(done)
                done += 1
    def key_back(raw, upstream):
        khat, factor = rms(raw.astype(F32))
        u = upstream * g1
        inner = jnp.mean(u * khat, axis=-1, keepdims=True)
        return factor * (u - khat * inner)

    for h in range(KH):
        back_arrived(1, h)
    for h in range(KH):
        cols = slice(h * HD, (h + 1) * HD)
        vcols = slice((KH + h) * HD, (KH + h + 1) * HD)
        dkvp[:, cols] = key_back(kvp[:, cols], fin[h, :, 0:HD]).astype(BF)
        dkvp[:, vcols] = fin[h, :, HD : 2 * HD].astype(BF)
    for h in range(KH):
        cols = slice(h * HD, (h + 1) * HD)
        vcols = slice((KH + h) * HD, (KH + h + 1) * HD)
        own = ew[0, h, :, 0 : 2 * HD] + returned(0, h)
        dkvr[:, cols] = key_back(kvr[:, cols], own[:, 0:HD]).astype(BF)
        dkvr[:, vcols] = own[:, HD : 2 * HD].astype(BF)

    while done < steps:
        gain_step(done)
        done += 1
    scales = [(total_rows * heads) ** (-0.5) for heads in (KH * SH, KH)]
    whole = red[steps][0:1, :]
    ngrad[0:1, :] = whole * scales[0]
    ngrad[1:2, :] = whole * (g0 / g1) * scales[1]

    def sent(n):
        k = n // KH
        h = n % KH

        @pl.when(me != 2 * NZ - 1)
        def _():
            fwd(k, h).wait_send()

        @pl.when(me != 0)
        def _():
            back(k + 1, h).wait_send()

        @pl.when((h >= half) & last)
        def _():
            fwd_over(k, h).wait_send()

        @pl.when((h >= half) & first_device)
        def _():
            back_over(k + 1, h).wait_send()

    loop(KH * REACH, sent)

    def ring_sent(m):
        gather_two(m).wait_send()
        scatter_two(m + 1).wait_send()

    loop(NZ // 2 - 1, ring_sent)

    def half_sent(m):
        for copy in (gather_one, gather_y, gather_side, scatter_one, scatter_y, scatter_side):
            copy(m).wait_send()

    loop(NZ // 2, half_sent)
    for i in range(steps):
        for j in range(len(partners[i])):
            gain_copy(i, j).wait_send()


def copy_out(*refs):
    for source, target in zip(refs[:5], refs[5:]):
        target[...] = source[...]


def per_device(mesh_shape, qp, qr, kvp, kvr, gp, gr, gains, lens):
    bits = [("resp", 1 << i) for i in range((mesh_shape["resp"] - 1).bit_length())]
    bits += [("prompt", 1 << i) for i in reversed(range((mesh_shape["prompt"] - 1).bit_length()))]
    rounds = tuple(tuple(bits[i : i + 3]) for i in range(0, len(bits), 3))
    total_rows = mesh_shape["prompt"] * mesh_shape["resp"] * (PROWS + RROWS)
    slots = len(rounds)
    vmem = pl.BlockSpec(memory_space=pltpu.VMEM)
    dma = pltpu.SemaphoreType.DMA
    block = (KH, RROWS, 2 * HD)
    pblock = (KH, PROWS, 2 * HD)
    scratch = [
        pltpu.VMEM((REACH + 1,) + block, BF),
        pltpu.VMEM((REACH, KH // 2, RROWS, 2 * HD), BF),
        pltpu.VMEM((NZ, 2) + pblock, BF),
        pltpu.VMEM((REACH,) + block, BF),
        pltpu.VMEM((REACH,) + block, BF),
        pltpu.VMEM((NZ - 1,) + pblock, BF),
        pltpu.VMEM((NZ - 1,) + pblock, BF),
        pltpu.VMEM((NZ // 2,) + pblock, BF),
        pltpu.VMEM((NZ // 2,) + pblock, BF),
        pltpu.VMEM((NZ // 2,) + pblock, BF),
        pltpu.VMEM((NZ // 2,) + pblock, BF),
        pltpu.VMEM(pblock, F32),
        pltpu.VMEM((KH, COLS, HD), BF),
        pltpu.VMEM((KH, HD, COLS), BF),
        pltpu.VMEM((KH, COLS, HD), BF),
        pltpu.VMEM((KH, HD, COLS), BF),
        pltpu.VMEM((KH, HD, COLS), F32),
        pltpu.VMEM((REACH + 1, KH, RROWS, RC), F32),
        pltpu.VMEM((REACH + 1, KH, RROWS, RC), F32),
        pltpu.VMEM((NZ // 2, KH, 4 * PROWS, COLS), F32),
        pltpu.VMEM((NZ // 2, KH, 4 * PROWS, COLS), F32),
        pltpu.VMEM((KH, 1, COLS), F32),
        pltpu.VMEM((KH, 1, COLS), F32),
        pltpu.VMEM((KH, 1, COLS), F32),
        pltpu.VMEM((REACH + 1, KH, 1, RC), F32),
        pltpu.VMEM((NZ // 2, KH, 1, COLS), F32),
        pltpu.VMEM((slots + 1, 8, HD), F32),
        pltpu.VMEM((slots, 7, 8, HD), F32),
        dma((REACH, KH)), dma((REACH, KH)), dma((REACH, KH)), dma((REACH, KH)),
        dma((REACH, KH)), dma((REACH, KH)), dma((REACH, KH)), dma((REACH, KH)),
        dma((NZ,)), dma((NZ,)), dma((NZ,)), dma((NZ,)),
        dma((NZ,)), dma((NZ,)), dma((NZ // 2,)), dma((NZ // 2,)), dma((NZ // 2,)), dma((NZ // 2,)),
        dma((slots, 7)), dma((slots, 7)),
    ]
    width = qp.shape[2]
    kvwidth = kvp.shape[2]
    outs = pl.pallas_call(
        functools.partial(kernel, rounds, total_rows),
        out_shape=(
            jax.ShapeDtypeStruct((PROWS, width), BF),
            jax.ShapeDtypeStruct((RROWS, width), BF),
            jax.ShapeDtypeStruct((PROWS, kvwidth), BF),
            jax.ShapeDtypeStruct((RROWS, kvwidth), BF),
            jax.ShapeDtypeStruct((2, HD), F32),
        ),
        in_specs=[vmem] * 7 + [pl.BlockSpec(memory_space=pltpu.SMEM)],
        out_specs=(vmem,) * 5,
        scratch_shapes=scratch,
        compiler_params=pltpu.CompilerParams(
            collective_id=0, has_side_effects=True, vmem_limit_bytes=62 * 1024 * 1024
        ),
    )(qp[0], qr[0], kvp[0], kvr[0], gp[0], gr[0], gains, lens)
    outs = pl.pallas_call(
        copy_out,
        out_shape=tuple(jax.ShapeDtypeStruct(out.shape, out.dtype) for out in outs),
        in_specs=[vmem] * 5,
        out_specs=(vmem,) * 5,
    )(*outs)
    return outs[0][None], outs[1][None], outs[2][None], outs[3][None], outs[4]


def solution(mesh):
    rows = P("prompt", "resp", None)
    return jax.shard_map(
        functools.partial(per_device, dict(mesh.shape)),
        mesh=mesh,
        in_specs=(rows,) * 6 + (P(), P("prompt", None)),
        out_specs=(rows,) * 4 + (P(),),
        check_vma=False,
    )
```
